256 devices in a mesh: dp: 16 (over y, x_hi, core), tensor: 16 (over x_lo, z).
Axes of the slice: x: 4 (x_hi: 2, x_lo: 2; x = x_hi * 2 + x_lo), y: 4, z: 8, core: 2. Of those that a mesh axis runs over, the one named last changes fastest.
Arguments:
- tokens: bfloat16 [8192, 2304], P('dp', 'tensor'), may hold values from -6 to 6
- cotangent: bfloat16 [8192, 2304], P('dp', 'tensor'), may hold values from -6 to 6
- prune_mask: int32 [18, 9216], P(None, 'tensor'), may hold values 0 or 1
- w_gate_up: bfloat16 [2, 2304, 9216], P(None, 'dp', 'tensor'), may hold values from -0.1875 to 0.1875
- w_down: bfloat16 [9216, 2304], P('tensor', 'dp'), may hold values from -0.0625 to 0.0625
- m_gate_up: float32 [2, 2304, 9216], P(None, 'dp', 'tensor'), may hold values from -2 to 2
- v_gate_up: float32 [2, 2304, 9216], P(None, 'dp', 'tensor'), may hold values from 0.01 to 0.3
- m_down: float32 [9216, 2304], P('tensor', 'dp'), may hold values from -2 to 2
- v_down: float32 [9216, 2304], P('tensor', 'dp'), may hold values from 0.01 to 0.3
Outputs:
- input_grad: bfloat16 [8192, 2304], P('dp', 'tensor')
- m_gate_up_new: float32 [2, 2304, 9216], P(None, 'dp', 'tensor')
- v_gate_up_new: float32 [2, 2304, 9216], P(None, 'dp', 'tensor')
- step_gate_up: float32 [2, 2304, 9216], P(None, 'dp', 'tensor')
- m_down_new: float32 [9216, 2304], P('tensor', 'dp')
- v_down_new: float32 [9216, 2304], P('tensor', 'dp')
- step_down: float32 [9216, 2304], P('tensor', 'dp')
The draws below stay inside these ranges and needn't reach their ends.
All inputs are finite; a program needn't handle non-finite values. No bound on the sum of `prune_mask` on one device may be relied on, other than what follows from the above.
Results may differ from the reference program's by a relative error of at most 0.005.
Values may be sent and summed in bfloat16 or wider, within the bound.
A program may use at most 128 MiB of HBM per device.

```python
import math
import jax
import jax.numpy as jnp

D = 2304
MBLK = 128
FF = 9216
TOKENS = 8192


def touch_ends(array, stream_key, least, high):
    longest = array.shape.index(max(array.shape))
    spots = []
    for shift in (0, 1):
        where = [jax.random.randint(jax.random.fold_in(stream_key, axis), (), 0, length) for axis, length in enumerate(array.shape)]
        where[longest] = (where[longest] + shift) % array.shape[longest]
        spots.append(tuple(where))
    return array.at[spots[0]].set(least).at[spots[1]].set(high)


def strengthened(entries, key, source, target, parts, factor):
    def block_of(position):
        return (jnp.arange(entries.shape[position]) // (entries.shape[position] // parts)).reshape((-1,) + (1,) * (entries.ndim - 1 - position))

    one_side = jax.random.permutation(key, parts)[block_of(target)]
    second = (block_of(target) + parts // 2) % parts
    return jnp.where((block_of(source) == one_side) | (block_of(source) == second), factor * entries, entries)


def block_levels(key, extent, shards, low, largest):
    def one(position, parts):
        heights = jax.random.uniform(jax.random.fold_in(jax.random.fold_in(key, 6), position), (parts,), jnp.float32, low / len(shards), largest / len(shards))
        return jnp.repeat(jnp.exp(heights), extent[position] // parts).reshape((-1,) + (1,) * (len(extent) - position - 1))

    loudness = one(*shards[0])
    for cut in shards[1:]:
        loudness = loudness * one(*cut)
    return loudness


def noise(stream_key, shape, width, limit, cuts=(), held_as=jnp.bfloat16):
    array = width * jax.random.normal(stream_key, shape, jnp.float32)
    if cuts:
        array = array * block_levels(stream_key, shape, cuts, -0.22, 0.18)
    return jnp.clip(array, -limit, limit).astype(held_as)


def bell_draw_with(key, shape, spread, most, cuts, heavy, dtype=jnp.bfloat16):
    result = spread * jax.random.normal(key, shape, jnp.float32)
    if cuts:
        result = result * block_levels(key, shape, cuts, -0.22, 0.18)
    return jnp.clip(strengthened(result, jax.random.fold_in(key, 3), *heavy), -most, most).astype(dtype)


def setup_inputs(seed: int = 0) -> dict:
    streams_of = jax.random.split(jax.random.key(seed), 10)
    return {
        "tokens": bell_draw_with(streams_of[0], (TOKENS, D), 1.0, 6.0, ((0, 16), (1, 16)), (0, 1, 16, 2.0)),
        "cotangent": bell_draw_with(streams_of[1], (TOKENS, D), 1.0, 6.0, ((0, 16), (1, 16)), (0, 1, 16, 2.0)),
        "prune_mask": touch_ends((jax.random.randint(streams_of[2], (D // MBLK, FF), 0, 4) < 3).astype(jnp.int32), jax.random.fold_in(streams_of[2], 1), 0, 1),
        "w_gate_up": bell_draw_with(streams_of[3], (2, D, FF), D ** -0.5, 0.1875, ((1, 16), (2, 16)), (2, 1, 16, 2.0)),
        "w_down": noise(streams_of[4], (FF, D), FF ** -0.5, 0.0625, ((0, 16), (1, 16))),
        "m_gate_up": noise(streams_of[5], (2, D, FF), 0.3, 2.0, ((1, 16), (2, 16)), jnp.float32),
        "v_gate_up": jnp.clip(jnp.exp(math.log(0.3) - 3.4011974 * jax.random.uniform(streams_of[6], (2, D, FF), jnp.float32) ** block_levels(streams_of[6], (2, D, FF), ((1, 16), (2, 16)), -0.2, 0.2)), 0.01, 0.3),
        "m_down": noise(streams_of[7], (FF, D), 0.3, 2.0, ((0, 16), (1, 16)), jnp.float32),
        "v_down": jnp.clip(jnp.exp(math.log(0.3) - 3.4011974 * jax.random.uniform(streams_of[8], (FF, D), jnp.float32) ** block_levels(streams_of[8], (FF, D), ((0, 16), (1, 16)), -0.2, 0.2)), 0.01, 0.3),
    }


def expand_mask(prune_mask):
    keep = prune_mask.astype(jnp.bfloat16)
    blocks, columns = keep.shape
    return jnp.broadcast_to(keep[:, None, :], (blocks, MBLK, columns)).reshape(blocks * MBLK, columns)

def adam_moments(first, second, grad):
    first_new = 0.9 * first + 0.1 * grad
    second_new = 0.95 * second + 0.05 * grad * grad
    return (first_new, second_new, first_new / (jnp.sqrt(second_new) + 1e-08))

def reference(tokens, cotangent, prune_mask, w_gate_up, w_down, m_gate_up, v_gate_up, m_down, v_down):
    keep_rows = expand_mask(prune_mask)
    eff_gate = w_gate_up[0] * keep_rows
    eff_up = w_gate_up[1] * keep_rows
    eff_down = w_down * keep_rows.T
    gate_value = jnp.dot(tokens, eff_gate, preferred_element_type=jnp.float32)
    up_value = jnp.dot(tokens, eff_up, preferred_element_type=jnp.float32)
    sigmoid_gate = jax.nn.sigmoid(gate_value)
    silu_gate = gate_value * sigmoid_gate
    hidden = (silu_gate * up_value).astype(jnp.bfloat16)
    hidden_grad = jnp.dot(cotangent, eff_down.T, preferred_element_type=jnp.float32)
    silu_slope = sigmoid_gate * (1.0 + gate_value * (1.0 - sigmoid_gate))
    gate_grad = (hidden_grad * up_value * silu_slope).astype(jnp.bfloat16)
    up_grad = (hidden_grad * silu_gate).astype(jnp.bfloat16)
    input_sum = jnp.dot(gate_grad, eff_gate.T, preferred_element_type=jnp.float32) + jnp.dot(up_grad, eff_up.T, preferred_element_type=jnp.float32)
    input_grad = input_sum.astype(jnp.bfloat16)
    grad_scale = jnp.float32(TOKENS) ** (-0.5)
    keep_float = keep_rows.astype(jnp.float32)
    grad_gate = jnp.dot(tokens.T, gate_grad, preferred_element_type=jnp.float32) * grad_scale * keep_float
    grad_up = jnp.dot(tokens.T, up_grad, preferred_element_type=jnp.float32) * grad_scale * keep_float
    grad_gate_up = jnp.stack([grad_gate, grad_up])
    grad_down = jnp.dot(hidden.T, cotangent, preferred_element_type=jnp.float32) * grad_scale * keep_float.T
    m_gate_up_new, v_gate_up_new, step_gate_up = adam_moments(m_gate_up, v_gate_up, grad_gate_up)
    m_down_new, v_down_new, step_down = adam_moments(m_down, v_down, grad_down)
    return (input_grad, m_gate_up_new, v_gate_up_new, step_gate_up, m_down_new, v_down_new, step_down)
```

```python
import functools
import jax
import jax.numpy as jnp
from jax import lax
from jax.experimental import pallas as pl
from jax.experimental.pallas import tpu as pltpu
from jax.sharding import PartitionSpec as P

BF = jnp.bfloat16
F32 = jnp.float32
MESH = pl.DeviceIdType.MESH

D = 2304
S = 144
T = 512
F = 576
MAIN = 512
GU = 1152
PK = 1792
CUTS = (((0, 80), (80, 64)), ((80, 64), (0, 80)))
COPIES = 80


def dot(a, b, ca, cb):
    return lax.dot_general(a, b, (((ca,), (cb,)), ((), ())), preferred_element_type=F32)


def rows(start, count, step=16):
    return pl.ds(pl.multiple_of(start, step), count)


def keep_of(mask_ref, dp):
    block = dp + dp // 8
    first = 128 - 16 * (dp % 8)
    row = lax.broadcasted_iota(jnp.int32, (S, F), 0)
    return jnp.where(row < first, mask_ref[pl.ds(block, 1), :], mask_ref[pl.ds(block + 1, 1), :])


def pack(ref, at, keep, gate, up, down):
    gate, up, down = (jnp.where(keep != 0, w.astype(F32), 0.0) for w in (gate, up, down))
    ref[at, 0:MAIN] = gate[:, :MAIN].astype(BF)
    ref[at, MAIN : 2 * MAIN] = up[:, :MAIN].astype(BF)
    ref[at, 2 * MAIN : GU] = jnp.concatenate([gate[:, MAIN:], up[:, MAIN:]], 1).astype(BF)
    ref[at, GU : GU + MAIN] = down[:, :MAIN].astype(BF)
    rest = down[:, MAIN:]
    ref[at, GU + MAIN : PK] = jnp.concatenate([rest, jnp.zeros_like(rest)], 1).astype(BF)


def add_rows(dst, to, n, *srcs):
    @pl.loop(0, n // 16)
    def _(i):
        at = rows(to + i * 16, 16)
        total = dst[at, :].astype(F32)
        for src, start in srcs:
            total += src[rows(start + i * 16, 16), :].astype(F32)
        dst[at, :] = total.astype(dst.dtype)


def grads_of(gate, up, hidden_grad):
    sig = jax.nn.sigmoid(gate)
    silu = gate * sig
    gate_grad = hidden_grad * up * (sig * (1.0 + gate * (1.0 - sig)))
    return gate_grad, hidden_grad * silu, silu * up


def hidden_pass(a, w, g, h):
    @pl.loop(0, 2)
    def _(m):
        tok = rows(m * 256, 256, 256)
        cot = rows(T + m * 256, 256, 256)

        @pl.loop(0, 2)
        def _(j):
            lo = rows(j * 256, 256, 256)
            hi = rows(MAIN + j * 256, 256, 256)
            gate = dot(a[:, tok], w[:, lo], 0, 0)
            up = dot(a[:, tok], w[:, hi], 0, 0)
            hg = dot(a[:, cot], w[:, rows(GU + j * 256, 256, 128)], 0, 0)
            gate_grad, up_grad, hidden = grads_of(gate, up, hg)
            g[tok, lo] = gate_grad.astype(BF)
            g[tok, hi] = up_grad.astype(BF)
            h[tok, lo] = hidden.astype(BF)

        both = dot(a[:, tok], w[:, 2 * MAIN : GU], 0, 0)
        hg = dot(a[:, cot], w[:, GU + MAIN : PK], 0, 0)
        gate_grad, up_grad, hidden = grads_of(both, pltpu.roll(both, 64, 1), hg)
        low = lax.broadcasted_iota(jnp.int32, (256, 128), 1) < 64
        g[tok, 2 * MAIN : GU] = jnp.where(low, gate_grad, pltpu.roll(up_grad, 64, 1)).astype(BF)
        h[tok, MAIN:640] = jnp.where(low, hidden, 0.0).astype(BF)


def body(tok_ref, cot_ref, mask_ref, wgu_ref, wd_ref, grad_ref, ig_ref,
         a, w, p, g, h, ig, sib, ya, yb, xb, za, zh, xl, send_sem, recv_sem):
    dp, tensor = lax.axis_index("dp"), lax.axis_index("tensor")
    y, hi, c = dp // 4, (dp // 2) % 2, dp % 2
    lo, z = tensor // 8, tensor % 8
    hk = (hi, 1 - hi)
    lk = (lo, 1 - lo)

    def dp_at(dy, k, flip=0):
        return (((y + dy) % 4) * 2 + hk[k]) * 2 + (1 - c if flip else c)

    def t_at(dz, k):
        return lk[k] * 8 + (z + dz) % 8

    up_y, down_y = (dp_at(1, 0), tensor), (dp_at(3, 0), tensor)
    up_z, down_z = (dp, t_at(1, 0)), (dp, t_at(7, 0))
    other_h, other_l, sibling = (dp_at(0, 1), tensor), (dp, t_at(0, 1)), (dp_at(0, 0, 1), tensor)
    ydev, zdev = (up_y, down_y), (up_z, down_z)

    barrier = pltpu.get_barrier_semaphore()
    partners = (up_y, down_y, up_z, down_z, other_h, other_l, sibling)
    for dev in partners:
        pl.semaphore_signal(barrier, inc=1, device_id=dev, device_id_type=MESH)

    sent = []

    def send(src, dst, dev):
        n = len(sent)
        copy = pltpu.make_async_remote_copy(
            src, dst, send_sem.at[n], recv_sem.at[n], device_id=dev, device_id_type=MESH
        )
        copy.start()
        sent.append(copy)
        return copy

    def got(*copies):
        for copy in copies:
            copy.wait_recv()

    def same(ref, start, count, dev):
        part = ref.at[rows(start, count)]
        return send(part, part, dev)

    def wrow(dy, k, flip=0):
        return dp_at(dy, k, flip) * S

    def arow(dz, k):
        return t_at(dz, k) * S

    own_a = rows(arow(0, 0), S)
    a[own_a, 0:T] = tok_ref[...].T
    a[own_a, T : 2 * T] = cot_ref[...].T
    keep = keep_of(mask_ref, dp)
    pack(w, rows(wrow(0, 0), S), keep, wgu_ref[0], wgu_ref[1], wd_ref[...].T)
    pl.semaphore_wait(barrier, len(partners))

    a_x = same(a, arow(0, 0), S, other_l)
    a0 = [same(a, arow(0, 0), S, d) for d in zdev]
    w0 = [same(w, wrow(0, 0), S, d) for d in ydev]
    w_x = same(w, wrow(0, 0), S, other_h)
    w_c = [same(w, wrow(0, 0), S, sibling)]

    def w_next(k, first):
        halves = []
        for way, (copy, dy) in enumerate(zip(first, (3, 1))):
            got(copy)
            start, count = CUTS[k][way]
            halves.append(same(w, wrow(dy, k) + start, count, ydev[way]))
            w_c.append(same(w, wrow(dy, k), S, sibling))
        return halves

    def w_last(k, halves):
        got(*halves)
        w_c.append(same(w, wrow(2, k), S, sibling))

    def a_next(k, copies, d):
        out = []
        for way, (copy, dz) in enumerate(zip(copies, (8 - d, d))):
            got(copy)
            start, count = CUTS[k][way] if d == 3 else (0, S)
            out.append(same(a, arow(dz, k) + start, count, zdev[way]))
        return out

    a1 = a_next(0, a0, 1)
    got(a_x)
    b0 = [same(a, arow(0, 1), S, d) for d in zdev]
    w1 = w_next(0, w0)
    got(w_x)
    v0 = [same(w, wrow(0, 1), S, d) for d in ydev]
    w_c.append(same(w, wrow(0, 1), S, sibling))
    a2 = a_next(0, a1, 2)
    b1 = a_next(1, b0, 1)
    w_last(0, w1)
    a3 = a_next(0, a2, 3)
    a_l = [same(a, arow(dz, 0), S, other_l) for dz in (5, 3)]
    v1 = w_next(1, v0)
    got(*a3)
    a_l.append(same(a, arow(4, 0), S, other_l))
    got(*b1)
    w_last(1, v1)
    got(*a_l, *w_c)

    hidden_pass(a, w, g, h)

    def weight_grads(dy):
        at = rows(((y + dy) % 4) * 4 * S, 4 * S)
        p[at, 0:GU] = dot(a[at, 0:T], g[...], 1, 0).astype(BF)
        p[at, GU:PK] = dot(a[at, T : 2 * T], h[...], 1, 0).astype(BF)
        out = {}
        for k in (1, 0):
            to = sib.at[rows((dp_at(dy, k) // 2) * S, S)]
            out[k] = send(p.at[rows(wrow(dy, k, 1), S)], to, sibling)
        return out

    def with_sibling(dy, k, copies):
        got(copies[k])
        add_rows(p, wrow(dy, k), S, (sib, (dp_at(dy, k) // 2) * S))

    def ya_row(k, way):
        return (k * 2 + way) * 80

    def yb_row(k, way):
        return (k * 2 + way) * S

    def y_far(k):
        out = []
        for way in (0, 1):
            start, count = CUTS[k][way]
            src = p.at[rows(wrow(2, k) + start, count)]
            out.append(send(src, ya.at[rows(ya_row(k, way), count)], ydev[way]))
        return out

    def y_near(k, way, part):
        start, count = CUTS[k][part]
        src = p.at[rows(wrow((1, 3)[way], k) + start, count)]
        return send(src, yb.at[rows(yb_row(k, way) + start, count)], ydev[way])

    def y_pass(k, far):
        out = []
        for way in (0, 1):
            got(far[way])
            start, count = CUTS[k][way]
            add_rows(p, wrow((1, 3)[way], k) + start, count, (ya, ya_row(k, way)))
            out.append(y_near(k, way, way))
        return out

    s2 = weight_grads(2)
    s1 = weight_grads(1)
    with_sibling(2, 1, s2)
    far1 = y_far(1)
    s3 = weight_grads(3)
    with_sibling(1, 1, s1)
    near1 = [y_near(1, 0, 1)]
    with_sibling(3, 1, s3)
    near1.append(y_near(1, 1, 0))
    with_sibling(2, 0, s2)
    far0 = y_far(0)
    s0 = weight_grads(0)

    @pl.loop(0, 2)
    def _(i):
        at = rows(i * 1152, 1152)
        ig[at, :] = dot(w[at, 0:GU], g[...], 1, 1).astype(BF)

    def za_row(k, way, step):
        return ((k * 2 + way) * 3 + step) * S

    def z_far(k):
        out = []
        for way in (0, 1):
            start, count = CUTS[k][way]
            src = ig.at[rows(arow(4, k) + start, count)]
            out.append(send(src, zh.at[rows((k * 2 + way) * 80, count)], zdev[way]))
        return out

    def z_pass(k, copies, d):
        out = []
        for way, dz in enumerate((d, 8 - d)):
            got(copies[way])
            if d == 3:
                start, count = CUTS[k][way]
                add_rows(ig, arow(dz, k) + start, count, (zh, (k * 2 + way) * 80))
            else:
                add_rows(ig, arow(dz, k), S, (za, za_row(k, way, 2 - d)))
            src = ig.at[rows(arow(dz, k), S)]
            out.append(send(src, za.at[rows(za_row(k, way, 3 - d), S)], zdev[way]))
        return out

    zc = {k: z_far(k) for k in (1, 0)}
    near1 += y_pass(1, far1)
    zc = {k: z_pass(k, zc[k], 3) for k in (1, 0)}
    with_sibling(1, 0, s1)
    near0 = [y_near(0, 0, 1)]
    with_sibling(3, 0, s3)
    near0.append(y_near(0, 1, 0))
    zc = {k: z_pass(k, zc[k], 2) for k in (1, 0)}
    near0 += y_pass(0, far0)
    zc = {k: z_pass(k, zc[k], 1) for k in (1, 0)}
    got(*zc[1])
    add_rows(ig, arow(0, 1), S, (za, za_row(1, 0, 2)), (za, za_row(1, 1, 2)))
    z_x = send(ig.at[rows(arow(0, 1), S)], xl, other_l)
    got(s0[1], *near1)
    own = (dp_at(0, 1) // 2) * S
    add_rows(p, wrow(0, 1), S, (sib, own), (yb, yb_row(1, 0)), (yb, yb_row(1, 1)))
    y_x = send(p.at[rows(wrow(0, 1), S)], xb, other_h)

    got(*zc[0], z_x)
    total = ig[rows(arow(0, 0), S), :].astype(F32) + xl[...].astype(F32)
    for way in (0, 1):
        total += za[rows(za_row(0, way, 2), S), :].astype(F32)
    ig_ref[...] = total
    got(s0[0], *near0, y_x)

    @pl.loop(0, S // 16)
    def _(i):
        at = rows(i * 16, 16)
        total = p[rows(wrow(0, 0) + i * 16, 16), :].astype(F32)
        total += sib[rows((dp_at(0, 0) // 2) * S + i * 16, 16), :].astype(F32)
        for way in (0, 1):
            total += yb[rows(yb_row(0, way) + i * 16, 16), :].astype(F32)
        grad_ref[at, :] = total + xb[at, :].astype(F32)

    for copy in sent:
        copy.wait_send()


def moments(m, v, grad):
    m_new = 0.9 * m + 0.1 * grad
    v_new = 0.95 * v + 0.05 * grad * grad
    return m_new, v_new, m_new / (jnp.sqrt(v_new) + 1e-8)


def finish(dp_ref, grad_ref, ig_ref, mask_ref, mgu_ref, vgu_ref, md_ref, vd_ref,
           out_ref, mgu_new, vgu_new, sgu, md_new, vd_new, sd):
    keep = keep_of(mask_ref, dp_ref[0])
    scale = jnp.float32(8192.0) ** -0.5
    rest = grad_ref[:, 2 * MAIN : GU]
    for k in (0, 1):
        tail = (rest if k == 0 else pltpu.roll(rest, 64, 1))[:, : F - MAIN]
        grad = jnp.concatenate([grad_ref[:, k * MAIN : (k + 1) * MAIN], tail], 1)
        grad = jnp.where(keep != 0, grad * scale, 0.0)
        mgu_new[k], vgu_new[k], sgu[k] = moments(mgu_ref[k], vgu_ref[k], grad)
    grad = jnp.where(keep != 0, grad_ref[:, GU : GU + F] * scale, 0.0).T
    md_new[...], vd_new[...], sd[...] = moments(md_ref[...], vd_ref[...], grad)
    out_ref[...] = ig_ref[...].T.astype(BF)


def on_device(tokens, cotangent, mask, wgu, wd, mgu, vgu, md, vd):
    vmem = pl.BlockSpec(memory_space=pltpu.VMEM)
    sds = jax.ShapeDtypeStruct
    grad, ig = pl.pallas_call(
        body,
        name="ffn_grads",
        out_shape=(sds((S, PK), F32), sds((S, T), F32)),
        in_specs=[vmem] * 5,
        out_specs=(vmem, vmem),
        scratch_shapes=[
            pltpu.VMEM((D, 2 * T), BF),
            pltpu.VMEM((D, PK), BF),
            pltpu.VMEM((D, PK), BF),
            pltpu.VMEM((T, GU), BF),
            pltpu.VMEM((T, 640), BF),
            pltpu.VMEM((D, T), BF),
            pltpu.VMEM((8 * S, PK), BF),
            pltpu.VMEM((4 * 80, PK), BF),
            pltpu.VMEM((4 * S, PK), BF),
            pltpu.VMEM((S, PK), BF),
            pltpu.VMEM((12 * S, T), BF),
            pltpu.VMEM((4 * 80, T), BF),
            pltpu.VMEM((S, T), BF),
            pltpu.SemaphoreType.DMA((COPIES,)),
            pltpu.SemaphoreType.DMA((COPIES,)),
        ],
        compiler_params=pltpu.CompilerParams(
            collective_id=0, has_side_effects=True, vmem_limit_bytes=58 << 20
        ),
    )(tokens, cotangent, mask, wgu, wd)
    dp = lax.axis_index("dp").astype(jnp.int32).reshape(1)
    big, down = sds((2, S, F), F32), sds((F, S), F32)
    return pl.pallas_call(
        finish,
        name="moments",
        out_shape=(sds((T, S), BF), big, big, big, down, down, down),
        in_specs=[pl.BlockSpec(memory_space=pltpu.SMEM)] + [vmem] * 7,
        out_specs=(vmem,) * 7,
        compiler_params=pltpu.CompilerParams(vmem_limit_bytes=40 << 20),
    )(dp, grad, ig, mask, mgu, vgu, md, vd)


def solution(mesh):
    return jax.shard_map(
        on_device,
        mesh=mesh,
        in_specs=(
            P("dp", "tensor"),
            P("dp", "tensor"),
            P(None, "tensor"),
            P(None, "dp", "tensor"),
            P("tensor", "dp"),
            P(None, "dp", "tensor"),
            P(None, "dp", "tensor"),
            P("tensor", "dp"),
            P("tensor", "dp"),
        ),
        out_specs=(
            P("dp", "tensor"),
            P(None, "dp", "tensor"),
            P(None, "dp", "tensor"),
            P(None, "dp", "tensor"),
            P("tensor", "dp"),
            P("tensor", "dp"),
            P("tensor", "dp"),
        ),
        check_vma=False,
    )
```

```python
import functools
import jax
import jax.numpy as jnp
from jax import lax
from jax.experimental import pallas as pl
from jax.experimental.pallas import tpu as pltpu
from jax.sharding import PartitionSpec as P

BF = jnp.bfloat16
F32 = jnp.float32
MESH = pl.DeviceIdType.MESH

D = 2304
S = 144
T = 512
F = 576
MAIN = 512
GU = 1152
PK = 1792
CUTS = (((0, 80), (80, 64)), ((80, 64), (0, 80)))
PARTS = ((0, 80), (80, 64))
WAYS = (0, 1)
COPIES = 96


def dot(a, b, ca, cb):
    return lax.dot_general(a, b, (((ca,), (cb,)), ((), ())), preferred_element_type=F32)


def rows(start, count, step=16):
    return pl.ds(pl.multiple_of(start, step), count)


def keep_of(mask_ref, dp):
    block = dp + dp // 8
    first = 128 - 16 * (dp % 8)
    row = lax.broadcasted_iota(jnp.int32, (S, F), 0)
    return jnp.where(row < first, mask_ref[pl.ds(block, 1), :], mask_ref[pl.ds(block + 1, 1), :])


def pack(ref, at, keep, gate, up, down):
    gate, up, down = (jnp.where(keep != 0, w.astype(F32), 0.0) for w in (gate, up, down))
    ref[at, 0:MAIN] = gate[:, :MAIN].astype(BF)
    ref[at, MAIN : 2 * MAIN] = up[:, :MAIN].astype(BF)
    ref[at, 2 * MAIN : GU] = jnp.concatenate([gate[:, MAIN:], up[:, MAIN:]], 1).astype(BF)
    ref[at, GU : GU + MAIN] = down[:, :MAIN].astype(BF)
    rest = down[:, MAIN:]
    ref[at, GU + MAIN : PK] = jnp.concatenate([rest, jnp.zeros_like(rest)], 1).astype(BF)


def add_rows(dst, to, n, *srcs):
    @pl.loop(0, n // 16)
    def _(i):
        at = rows(to + i * 16, 16)
        total = dst[at, :].astype(F32)
        for src, start in srcs:
            total += src[rows(start + i * 16, 16), :].astype(F32)
        dst[at, :] = total.astype(dst.dtype)


def grads_of(gate, up, hidden_grad):
    sig = jax.nn.sigmoid(gate)
    silu = gate * sig
    gate_grad = hidden_grad * up * (sig * (1.0 + gate * (1.0 - sig)))
    return gate_grad, hidden_grad * silu, silu * up


def hidden_pass(a, w, g, h):
    @pl.loop(0, 2)
    def _(m):
        tok = rows(m * 256, 256, 256)
        cot = rows(T + m * 256, 256, 256)

        @pl.loop(0, 2)
        def _(j):
            lo = rows(j * 256, 256, 256)
            hi = rows(MAIN + j * 256, 256, 256)
            gate = dot(a[:, tok], w[:, lo], 0, 0)
            up = dot(a[:, tok], w[:, hi], 0, 0)
            hg = dot(a[:, cot], w[:, rows(GU + j * 256, 256, 128)], 0, 0)
            gate_grad, up_grad, hidden = grads_of(gate, up, hg)
            g[tok, lo] = gate_grad.astype(BF)
            g[tok, hi] = up_grad.astype(BF)
            h[tok, lo] = hidden.astype(BF)

        both = dot(a[:, tok], w[:, 2 * MAIN : GU], 0, 0)
        hg = dot(a[:, cot], w[:, GU + MAIN : PK], 0, 0)
        gate_grad, up_grad, hidden = grads_of(both, pltpu.roll(both, 64, 1), hg)
        low = lax.broadcasted_iota(jnp.int32, (256, 128), 1) < 64
        g[tok, 2 * MAIN : GU] = jnp.where(low, gate_grad, pltpu.roll(up_grad, 64, 1)).astype(BF)
        h[tok, MAIN:640] = jnp.where(low, hidden, 0.0).astype(BF)


def body(tok_hbm, cot_hbm, mask_hbm, wgu_hbm, wd_hbm, grad_ref, ig_ref,
         mask_ref, wgu_ref, wd_ref, in_sem, a, w, p, g, h, ig, sib, ya, yb, xb, za, zh, xl, send_sem, recv_sem):
    dp, tensor = lax.axis_index("dp"), lax.axis_index("tensor")
    y, hi, c = dp // 4, (dp // 2) % 2, dp % 2
    lo, z = tensor // 8, tensor % 8
    hk = (hi, 1 - hi)
    lk = (lo, 1 - lo)

    def dp_at(dy, k, flip=0):
        return (((y + dy) % 4) * 2 + hk[k]) * 2 + (1 - c if flip else c)

    def t_at(dz, k):
        return lk[k] * 8 + (z + dz) % 8

    up_y, down_y = (dp_at(1, 0), tensor), (dp_at(3, 0), tensor)
    up_z, down_z = (dp, t_at(1, 0)), (dp, t_at(7, 0))
    other_h, other_l, sibling = (dp_at(0, 1), tensor), (dp, t_at(0, 1)), (dp_at(0, 0, 1), tensor)
    ydev, zdev = (up_y, down_y), (up_z, down_z)

    own_a = rows((lo * 8 + z) * S, S)
    loads = [
        pltpu.make_async_copy(src, dst, in_sem.at[n])
        for n, (src, dst) in enumerate((
            (tok_hbm, a.at[own_a, pl.ds(0, T)]),
            (cot_hbm, a.at[own_a, pl.ds(T, T)]),
            (mask_hbm, mask_ref),
            (wgu_hbm, wgu_ref),
            (wd_hbm, wd_ref),
        ))
    ]
    for load in loads:
        load.start()

    barrier = pltpu.get_barrier_semaphore()
    partners = (up_y, down_y, up_z, down_z, other_h, other_l, sibling)
    for dev in partners:
        pl.semaphore_signal(barrier, inc=1, device_id=dev, device_id_type=MESH)

    sent = []

    def send(src, dst, dev):
        n = len(sent)
        copy = pltpu.make_async_remote_copy(
            src, dst, send_sem.at[n], recv_sem.at[n], device_id=dev, device_id_type=MESH
        )
        copy.start()
        sent.append(copy)
        return copy

    def drain():
        for copy in sent:
            copy.wait_send()

    def got(*copies):
        for copy in copies:
            copy.wait_recv()

    def same(ref, start, count, dev):
        part = ref.at[rows(start, count)]
        return send(part, part, dev)

    def wrow(dy, k, flip=0):
        return dp_at(dy, k, flip) * S

    def arow(dz, k):
        return t_at(dz, k) * S

    def part_of(ref, start, part, dev):
        return same(ref, start + PARTS[part][0], PARTS[part][1], dev)

    def to_sibling(dy, k):
        w_c.append(same(w, wrow(dy, k), S, sibling))

    for load in loads[:2]:
        load.wait()
    pl.semaphore_wait(barrier, len(partners))
    w_c = []
    a_x = same(a, arow(0, 0), S, other_l)
    a0, a1, a2, a3, b0, b1 = {}, {}, {}, {}, {}, {}
    w0, w1, v0, v1 = {}, {}, {}, {}
    for turn in (0, 1):
        for way in WAYS:
            a0[way, turn ^ way] = part_of(a, arow(0, 0), turn ^ way, zdev[way])
    for load in loads[2:]:
        load.wait()
    pack(w, rows(wrow(0, 0), S), keep_of(mask_ref, dp), wgu_ref[0], wgu_ref[1], wd_ref[...])
    for turn in (0, 1):
        for way in WAYS:
            w0[way, turn ^ way] = part_of(w, wrow(0, 0), turn ^ way, ydev[way])
    w_x = [part_of(w, wrow(0, 0), part, other_h) for part in (0, 1)]
    to_sibling(0, 0)

    def a_next(copies, out, k, d, part, way):
        got(copies[way, part])
        out[way, part] = part_of(a, arow((8 - d, d)[way], k), part, zdev[way])

    def w_next(copies, out, k):
        for way in WAYS:
            part = way ^ k
            got(copies[way, part])
            out[way, part] = part_of(w, wrow((3, 1)[way], k), part, ydev[way])

    def w_rest(copies, k):
        for way in WAYS:
            got(copies[way, 1 - way ^ k])
            to_sibling((3, 1)[way], k)

    def w_last(copies, k):
        got(*copies.values())
        to_sibling(2, k)

    for way in WAYS:
        a_next(a0, a1, 0, 1, way, way)
    w_next(w0, w1, 0)
    for way in WAYS:
        a_next(a0, a1, 0, 1, 1 - way, way)
    for way in WAYS:
        a_next(a1, a2, 0, 2, way, way)
    w_rest(w0, 0)
    for way in WAYS:
        a_next(a1, a2, 0, 2, 1 - way, way)
    got(a_x)
    for part in (0, 1):
        for way in WAYS:
            b0[way, part] = part_of(a, arow(0, 1), part, zdev[way])
    for part in (0, 1):
        got(w_x[part])
        for way in WAYS:
            v0[way, part] = part_of(w, wrow(0, 1), part, ydev[way])
    to_sibling(0, 1)
    a_l = []
    for way in WAYS:
        a_next(a2, a3, 0, 3, way, way)
        a_l.append(part_of(a, arow((5, 3)[way], 0), way, other_l))
    w_last(w1, 0)
    for way in WAYS:
        got(a2[way, 1 - way])
        a_l.append(part_of(a, arow((5, 3)[way], 0), 1 - way, other_l))
    for way in WAYS:
        a_next(b0, b1, 1, 1, 0, way)
    for way in WAYS:
        got(a3[way, way])
        a_l.append(part_of(a, arow(4, 0), way, other_l))
    w_next(v0, v1, 1)
    for way in WAYS:
        a_next(b0, b1, 1, 1, 1, way)
    w_rest(v0, 1)
    got(*b1.values())
    w_last(v1, 1)
    got(*a_l, *w_c)

    hidden_pass(a, w, g, h)

    def weight_grads(dy):
        at = rows(((y + dy) % 4) * 4 * S, 4 * S)
        p[at, 0:GU] = dot(a[at, 0:T], g[...], 1, 0).astype(BF)
        p[at, GU:PK] = dot(a[at, T : 2 * T], h[...], 1, 0).astype(BF)
        out = {}
        for k in (1, 0):
            to = sib.at[rows((dp_at(dy, k) // 2) * S, S)]
            out[k] = send(p.at[rows(wrow(dy, k, 1), S)], to, sibling)
        return out

    def with_sibling(dy, k, copies):
        got(copies[k])
        add_rows(p, wrow(dy, k), S, (sib, (dp_at(dy, k) // 2) * S))

    def ya_row(k, way):
        return (k * 2 + way) * 80

    def yb_row(k, way):
        return (k * 2 + way) * S

    def y_far(k):
        out = []
        for way in (0, 1):
            start, count = CUTS[k][way]
            src = p.at[rows(wrow(2, k) + start, count)]
            out.append(send(src, ya.at[rows(ya_row(k, way), count)], ydev[way]))
        return out

    def y_near(k, way, part):
        start, count = CUTS[k][part]
        src = p.at[rows(wrow((1, 3)[way], k) + start, count)]
        return send(src, yb.at[rows(yb_row(k, way) + start, count)], ydev[way])

    def y_pass(k, far):
        out = []
        for way in (0, 1):
            got(far[way])
            start, count = CUTS[k][way]
            add_rows(p, wrow((1, 3)[way], k) + start, count, (ya, ya_row(k, way)))
            out.append(y_near(k, way, way))
        return out

    def input_grad(k):
        at = rows(lk[k] * 1152, 1152)
        ig[at, :] = dot(w[at, 0:GU], g[...], 1, 1).astype(BF)

    def za_row(k, way, step):
        return ((k * 2 + way) * 3 + step) * S

    def z_far(k):
        out = []
        for way in (0, 1):
            start, count = CUTS[k][way]
            src = ig.at[rows(arow(4, k) + start, count)]
            out.append(send(src, zh.at[rows((k * 2 + way) * 80, count)], zdev[way]))
        return out

    def z_pass(k, copies, d):
        out = []
        for way, dz in enumerate((d, 8 - d)):
            got(copies[way])
            if d == 3:
                start, count = CUTS[k][way]
                add_rows(ig, arow(dz, k) + start, count, (zh, (k * 2 + way) * 80))
            else:
                add_rows(ig, arow(dz, k), S, (za, za_row(k, way, 2 - d)))
            src = ig.at[rows(arow(dz, k), S)]
            out.append(send(src, za.at[rows(za_row(k, way, 3 - d), S)], zdev[way]))
        return out

    s2 = weight_grads(2)
    s1 = weight_grads(1)
    with_sibling(2, 1, s2)
    far1 = y_far(1)
    s3 = weight_grads(3)
    with_sibling(1, 1, s1)
    near1 = [y_near(1, 0, 1)]
    input_grad(1)
    zc = {1: z_far(1)}
    with_sibling(3, 1, s3)
    near1.append(y_near(1, 1, 0))
    with_sibling(2, 0, s2)
    input_grad(0)
    zc[0] = z_far(0)
    near1 += y_pass(1, far1)
    far0 = y_far(0)
    with_sibling(1, 0, s1)
    near0 = [y_near(0, 0, 1)]
    with_sibling(3, 0, s3)
    near0.append(y_near(0, 1, 0))
    zc[1] = z_pass(1, zc[1], 3)
    s0 = weight_grads(0)
    zc[0] = z_pass(0, zc[0], 3)
    zc[1] = z_pass(1, zc[1], 2)
    zc[0] = z_pass(0, zc[0], 2)
    got(s0[1], *near1)
    own = (dp_at(0, 1) // 2) * S
    add_rows(p, wrow(0, 1), S, (sib, own), (yb, yb_row(1, 0)), (yb, yb_row(1, 1)))
    y_x = send(p.at[rows(wrow(0, 1), S)], xb, other_h)
    near0 += y_pass(0, far0)
    zc[1] = z_pass(1, zc[1], 1)
    zc[0] = z_pass(0, zc[0], 1)
    got(*zc[1])
    add_rows(ig, arow(0, 1), S, (za, za_row(1, 0, 2)), (za, za_row(1, 1, 2)))
    z_x = send(ig.at[rows(arow(0, 1), S)], xl, other_l)

    got(*zc[0], z_x)
    total = ig[rows(arow(0, 0), S), :].astype(F32) + xl[...].astype(F32)
    for way in (0, 1):
        total += za[rows(za_row(0, way, 2), S), :].astype(F32)
    ig_ref[...] = total
    got(s0[0], *near0, y_x)

    @pl.loop(0, S // 16)
    def _(i):
        at = rows(i * 16, 16)
        total = p[rows(wrow(0, 0) + i * 16, 16), :].astype(F32)
        total += sib[rows((dp_at(0, 0) // 2) * S + i * 16, 16), :].astype(F32)
        for way in (0, 1):
            total += yb[rows(yb_row(0, way) + i * 16, 16), :].astype(F32)
        grad_ref[at, :] = total + xb[at, :].astype(F32)

    drain()


def moments(m, v, grad):
    m_new = 0.9 * m + 0.1 * grad
    v_new = 0.95 * v + 0.05 * grad * grad
    return m_new, v_new, m_new / (jnp.sqrt(v_new) + 1e-8)


def finish(dp_ref, grad_hbm, ig_hbm, mask_hbm, mgu_hbm, vgu_hbm, md_hbm, vd_hbm,
           out_hbm, mgu_new, vgu_new, sgu_new, md_new, vd_new, sd_new,
           grad_ref, ig_ref, mask, out, old, new, in_sem, out_sem):
    firsts = (mgu_hbm.at[0], mgu_hbm.at[1], md_hbm)
    seconds = (vgu_hbm.at[0], vgu_hbm.at[1], vd_hbm)
    loads = [
        pltpu.make_async_copy(mask_hbm, mask, in_sem.at[6]),
        pltpu.make_async_copy(grad_hbm, grad_ref, in_sem.at[7]),
        pltpu.make_async_copy(ig_hbm, ig_ref, in_sem.at[8]),
    ]
    for k in range(3):
        loads.append(pltpu.make_async_copy(firsts[k], old.at[2 * k], in_sem.at[2 * k]))
        loads.append(pltpu.make_async_copy(seconds[k], old.at[2 * k + 1], in_sem.at[2 * k + 1]))
    for load in loads:
        load.start()
    loads[2].wait()
    out[...] = ig_ref[...].astype(BF)
    stores = [pltpu.make_async_copy(out, out_hbm, out_sem.at[9])]
    stores[0].start()
    loads[0].wait()
    loads[1].wait()
    scale = jnp.float32(8192.0) ** -0.5
    keep = jnp.where(keep_of(mask, dp_ref[0]) != 0, scale, 0.0)
    rest = grad_ref[:, 2 * MAIN : GU]
    results = ((mgu_new.at[0], vgu_new.at[0], sgu_new.at[0]),
               (mgu_new.at[1], vgu_new.at[1], sgu_new.at[1]),
               (md_new, vd_new, sd_new))
    for k in range(3):
        if k < 2:
            tail = (rest if k == 0 else pltpu.roll(rest, 64, 1))[:, : F - MAIN]
            grad = jnp.concatenate([grad_ref[:, k * MAIN : (k + 1) * MAIN], tail], 1)
        else:
            grad = grad_ref[:, GU : GU + F]
        loads[3 + 2 * k].wait()
        loads[4 + 2 * k].wait()
        new[3 * k], new[3 * k + 1], new[3 * k + 2] = moments(
            old[2 * k], old[2 * k + 1], grad * keep
        )
        for n in range(3):
            store = pltpu.make_async_copy(new.at[3 * k + n], results[k][n], out_sem.at[3 * k + n])
            store.start()
            stores.append(store)
    for store in stores:
        store.wait()


VMEM = pl.BlockSpec(memory_space=pltpu.VMEM)
HBM = pl.BlockSpec(memory_space=pltpu.HBM)
sds = jax.ShapeDtypeStruct


def ffn(tokens, cotangent, mask, wgu, wd):
    return pl.pallas_call(
        body,
        name="ffn_grads",
        out_shape=(sds((S, PK), F32), sds((S, T), F32)),
        in_specs=[HBM] * 5,
        out_specs=(VMEM, VMEM),
        scratch_shapes=[
            pltpu.VMEM(mask.shape, jnp.int32),
            pltpu.VMEM(wgu.shape, BF),
            pltpu.VMEM(wd.shape, BF),
            pltpu.SemaphoreType.DMA((5,)),
            pltpu.VMEM((D, 2 * T), BF),
            pltpu.VMEM((D, PK), BF),
            pltpu.VMEM((D, PK), BF),
            pltpu.VMEM((T, GU), BF),
            pltpu.VMEM((T, 640), BF),
            pltpu.VMEM((D, T), BF),
            pltpu.VMEM((8 * S, PK), BF),
            pltpu.VMEM((4 * 80, PK), BF),
            pltpu.VMEM((4 * S, PK), BF),
            pltpu.VMEM((S, PK), BF),
            pltpu.VMEM((12 * S, T), BF),
            pltpu.VMEM((4 * 80, T), BF),
            pltpu.VMEM((S, T), BF),
            pltpu.SemaphoreType.DMA((COPIES,)),
            pltpu.SemaphoreType.DMA((COPIES,)),
        ],
        compiler_params=pltpu.CompilerParams(
            collective_id=0, has_side_effects=True, vmem_limit_bytes=62 << 20
        ),
    )(tokens, cotangent, mask, wgu, wd)


def on_device(tokens, cotangent, mask, wgu, wd, mgu, vgu, md, vd):
    grad, ig = ffn(tokens.T, cotangent.T, mask, wgu, wd.T)
    dp = lax.axis_index("dp").astype(jnp.int32).reshape(1)
    big, down = sds((2, S, F), F32), sds((S, F), F32)
    out = pl.pallas_call(
        finish,
        name="moments",
        out_shape=(sds((S, T), BF), big, big, big, down, down, down),
        in_specs=[pl.BlockSpec(memory_space=pltpu.SMEM)] + [HBM] * 7,
        out_specs=(HBM,) * 7,
        scratch_shapes=[
            pltpu.VMEM((S, PK), F32),
            pltpu.VMEM((S, T), F32),
            pltpu.VMEM(mask.shape, jnp.int32),
            pltpu.VMEM((S, T), BF),
            pltpu.VMEM((6, S, F), F32),
            pltpu.VMEM((9, S, F), F32),
            pltpu.SemaphoreType.DMA((9,)),
            pltpu.SemaphoreType.DMA((10,)),
        ],
        compiler_params=pltpu.CompilerParams(vmem_limit_bytes=62 << 20),
    )(dp, grad, ig, mask, mgu, vgu, md.T, vd.T)
    return (out[0].T, *out[1:4], *(x.T for x in out[4:]))


def solution(mesh):
    return jax.shard_map(
        on_device,
        mesh=mesh,
        in_specs=(
            P("dp", "tensor"),
            P("dp", "tensor"),
            P(None, "tensor"),
            P(None, "dp", "tensor"),
            P("tensor", "dp"),
            P(None, "dp", "tensor"),
            P(None, "dp", "tensor"),
            P("tensor", "dp"),
            P("tensor", "dp"),
        ),
        out_specs=(
            P("dp", "tensor"),
            P(None, "dp", "tensor"),
            P(None, "dp", "tensor"),
            P(None, "dp", "tensor"),
            P("tensor", "dp"),
            P("tensor", "dp"),
            P("tensor", "dp"),
        ),
        check_vma=False,
    )
```

```python
import functools
import jax
import jax.numpy as jnp
from jax import lax
from jax.experimental import pallas as pl
from jax.experimental.pallas import tpu as pltpu
from jax.sharding import PartitionSpec as P

BF = jnp.bfloat16
F32 = jnp.float32
MESH = pl.DeviceIdType.MESH

D = 2304
S = 144
T = 512
F = 576
MAIN = 512
PK = 1792
HALF = ((0, 768), (768, 1024))
GLANES = ((0, 512), (512, 640))
HLANES = ((0, 256), (256, 384))
CUTS = (((0, 80), (80, 64)), ((80, 64), (0, 80)))
PARTS = ((0, 80), (80, 64))
WAYS = (0, 1)
COPIES = 128


def dot(a, b, ca, cb):
    return lax.dot_general(a, b, (((ca,), (cb,)), ((), ())), preferred_element_type=F32)


def rows(start, count, step=16):
    return pl.ds(pl.multiple_of(start, step), count)


def keep_of(mask_ref, dp):
    block = dp + dp // 8
    first = 128 - 16 * (dp % 8)
    row = lax.broadcasted_iota(jnp.int32, (S, F), 0)
    return jnp.where(row < first, mask_ref[pl.ds(block, 1), :], mask_ref[pl.ds(block + 1, 1), :])


def pack(ref, at, keep, gate, up, down):
    gate, up, down = (jnp.where(keep != 0, w.astype(F32), 0.0) for w in (gate, up, down))
    at_lane = 0
    rest = jnp.concatenate([gate[:, MAIN:], up[:, MAIN:]], 1)
    last = jnp.concatenate([down[:, MAIN:], jnp.zeros_like(down[:, MAIN:])], 1)
    for part in (gate[:, :256], up[:, :256], down[:, :256], gate[:, 256:MAIN], up[:, 256:MAIN],
                 rest, down[:, 256:MAIN], last):
        ref[at, at_lane : at_lane + part.shape[1]] = part.astype(BF)
        at_lane += part.shape[1]


def add_rows(dst, to, n, lanes, *srcs):
    cols = pl.ds(*lanes)

    @pl.loop(0, n // 16)
    def _(i):
        at = rows(to + i * 16, 16)
        total = dst[at, cols].astype(F32)
        for src, start in srcs:
            total += src[rows(start + i * 16, 16), cols].astype(F32)
        dst[at, cols] = total.astype(dst.dtype)


def grads_of(gate, up, hidden_grad):
    sig = jax.nn.sigmoid(gate)
    silu = gate * sig
    gate_grad = hidden_grad * up * (sig * (1.0 + gate * (1.0 - sig)))
    return gate_grad, hidden_grad * silu, silu * up


def hidden_pass(a, w, g, h, half, m):
    tok = rows(m * 256, 256, 256)
    cot = rows(T + m * 256, 256, 256)
    first, (gl, gn), (hl, hn) = HALF[half][0], GLANES[half], HLANES[half]
    both = dot(a[:, tok], w[:, first : first + gn], 0, 0)
    hg = dot(a[:, cot], w[:, first + gn : first + gn + hn], 0, 0)
    gate_grad, up_grad, hidden = grads_of(both[:, :256], both[:, 256:512], hg[:, :256])
    g[tok, gl : gl + 256] = gate_grad.astype(BF)
    g[tok, gl + 256 : gl + 512] = up_grad.astype(BF)
    h[tok, hl : hl + 256] = hidden.astype(BF)
    if half == 1:
        both, hg = both[:, 512:], hg[:, 256:]
        gate_grad, up_grad, hidden = grads_of(both, pltpu.roll(both, 64, 1), hg)
        low = lax.broadcasted_iota(jnp.int32, (256, 128), 1) < 64
        g[tok, 1024:1152] = jnp.where(low, gate_grad, pltpu.roll(up_grad, 64, 1)).astype(BF)
        h[tok, 512:640] = jnp.where(low, hidden, 0.0).astype(BF)


def body(tok_hbm, cot_hbm, mask_hbm, wgu_hbm, wd_hbm, grad_ref, ig_ref,
         mask_ref, wgu_ref, wd_ref, in_sem, a, w, p, g, h, ig, sib, ya, yb, xb, xq, za, zh, xl, send_sem, recv_sem):
    dp, tensor = lax.axis_index("dp"), lax.axis_index("tensor")
    y, hi, c = dp // 4, (dp // 2) % 2, dp % 2
    lo, z = tensor // 8, tensor % 8
    hk = (hi, 1 - hi)
    lk = (lo, 1 - lo)

    def dp_at(dy, k, flip=0):
        return (((y + dy) % 4) * 2 + hk[k]) * 2 + (1 - c if flip else c)

    def t_at(dz, k):
        return lk[k] * 8 + (z + dz) % 8

    up_y, down_y = (dp_at(1, 0), tensor), (dp_at(3, 0), tensor)
    up_z, down_z = (dp, t_at(1, 0)), (dp, t_at(7, 0))
    other_h, other_l, sibling = (dp_at(0, 1), tensor), (dp, t_at(0, 1)), (dp_at(0, 0, 1), tensor)
    ydev, zdev = (up_y, down_y), (up_z, down_z)

    own_a = rows((lo * 8 + z) * S, S)
    loads = [
        pltpu.make_async_copy(src, dst, in_sem.at[n])
        for n, (src, dst) in enumerate((
            (tok_hbm, a.at[own_a, pl.ds(0, T)]),
            (cot_hbm, a.at[own_a, pl.ds(T, T)]),
            (mask_hbm, mask_ref),
            (wgu_hbm, wgu_ref),
            (wd_hbm, wd_ref),
        ))
    ]
    for load in loads:
        load.start()

    barrier = pltpu.get_barrier_semaphore()
    partners = (up_y, down_y, up_z, down_z, other_h, other_l, sibling)
    for dev in partners:
        pl.semaphore_signal(barrier, inc=1, device_id=dev, device_id_type=MESH)

    sent = []

    def send(src, dst, dev):
        n = len(sent)
        copy = pltpu.make_async_remote_copy(
            src, dst, send_sem.at[n], recv_sem.at[n], device_id=dev, device_id_type=MESH
        )
        copy.start()
        sent.append(copy)
        return copy

    def drain():
        for copy in sent:
            copy.wait_send()

    def got(*copies):
        for copy in copies:
            copy.wait_recv()

    def same(ref, start, count, dev):
        part = ref.at[rows(start, count)]
        return send(part, part, dev)

    def wrow(dy, k, flip=0):
        return dp_at(dy, k, flip) * S

    def arow(dz, k):
        return t_at(dz, k) * S

    def part(ref, start, count, half):
        return ref.at[rows(start, count), pl.ds(*HALF[half])]

    def part_of(ref, start, part, dev):
        return same(ref, start + PARTS[part][0], PARTS[part][1], dev)

    def to_sibling(dy, k):
        w_c.append(same(w, wrow(dy, k), S, sibling))

    for load in loads:
        load.wait()
    pack(w, rows(wrow(0, 0), S), keep_of(mask_ref, dp), wgu_ref[0], wgu_ref[1], wd_ref[...])
    pl.semaphore_wait(barrier, len(partners))
    core_w = ([], [])
    a_x = same(a, arow(0, 0), S, other_l)
    a0, a1, a2, a3, b0, b1 = {}, {}, {}, {}, {}, {}
    w0, w1, v0, v1, w_x = {}, {}, {}, {}, {}

    def w_send(start, count, half, dev):
        src = part(w, start, count, half)
        return send(src, src, dev)

    def to_sibling(dy, k, half):
        core_w[half].append(w_send(wrow(dy, k), S, half, sibling))

    def w_start(out, k, half):
        for way in WAYS:
            out[way, half] = w_send(wrow(0, k), S, half, ydev[way])

    def w_next(copies, out, k, half):
        for way in WAYS:
            got(copies[way, half])
            start, count = CUTS[k][way]
            out[way, half] = w_send(wrow((3, 1)[way], k) + start, count, half, ydev[way])
            to_sibling((3, 1)[way], k, half)

    def w_last(copies, k, half):
        got(copies[0, half], copies[1, half])
        to_sibling(2, k, half)

    def a_next(copies, out, k, d, part, way):
        got(copies[way, part])
        out[way, part] = part_of(a, arow((8 - d, d)[way], k), part, zdev[way])

    for turn in (0, 1):
        for way in WAYS:
            a0[way, turn ^ way] = part_of(a, arow(0, 0), turn ^ way, zdev[way])
    for half in (0, 1):
        w_start(w0, 0, half)
        w_x[half] = w_send(wrow(0, 0), S, half, other_h)
    for half in (0, 1):
        to_sibling(0, 0, half)
    for way in WAYS:
        a_next(a0, a1, 0, 1, way, way)
    w_next(w0, w1, 0, 0)
    for way in WAYS:
        a_next(a0, a1, 0, 1, 1 - way, way)
    for way in WAYS:
        a_next(a1, a2, 0, 2, way, way)
    w_next(w0, w1, 0, 1)
    got(w_x[0])
    w_start(v0, 1, 0)
    to_sibling(0, 1, 0)
    for way in WAYS:
        a_next(a1, a2, 0, 2, 1 - way, way)
    got(a_x)
    for turn in (0, 1):
        for way in WAYS:
            b0[way, turn] = part_of(a, arow(0, 1), turn, zdev[way])
    a_l = []
    for way in WAYS:
        a_next(a2, a3, 0, 3, way, way)
        a_l.append(part_of(a, arow((5, 3)[way], 0), way, other_l))
    got(w_x[1])
    w_start(v0, 1, 1)
    to_sibling(0, 1, 1)
    w_last(w1, 0, 0)
    for way in WAYS:
        got(a2[way, 1 - way])
        a_l.append(part_of(a, arow((5, 3)[way], 0), 1 - way, other_l))
    w_last(w1, 0, 1)
    for way in WAYS:
        a_next(b0, b1, 1, 1, 0, way)
    for way in WAYS:
        got(a3[way, way])
        a_l.append(part_of(a, arow(4, 0), way, other_l))
    w_next(v0, v1, 1, 0)
    for way in WAYS:
        a_next(b0, b1, 1, 1, 1, way)
    w_next(v0, v1, 1, 1)
    w_last(v1, 1, 0)
    got(*b1.values())
    w_last(v1, 1, 1)
    got(*a_l, *core_w[0])

    def sib_row(dy, k):
        return (dp_at(dy, k) // 2) * S

    def yb_row(k, way):
        return (k * 2 + way) * S

    def weight_product(at, half):
        first, (gl, gn), (hl, hn) = HALF[half][0], GLANES[half], HLANES[half]
        p[at, first : first + gn] = dot(a[at, 0:T], g[:, gl : gl + gn], 1, 0).astype(BF)
        p[at, first + gn : first + gn + hn] = dot(
            a[at, T : 2 * T], h[:, hl : hl + hn], 1, 0
        ).astype(BF)

    def core_copy(dy, k, half, n):
        return pltpu.make_async_remote_copy(
            part(p, wrow(dy, k, 1), S, half), part(sib, sib_row(dy, k), S, half),
            send_sem.at[n], recv_sem.at[n], device_id=sibling, device_id_type=MESH,
        )

    def weight_grads(dys, k, half):
        n0 = len(sent)
        step = (dys[1] - dys[0]) % 4 if len(dys) > 1 else 0
        third = dys[2] - dys[0] - 2 * step if len(dys) > 2 else 0
        for q, dy in enumerate(dys):
            copy = core_copy(dy, k, half, n0 + q)
            sent.append(copy)
            core[dy, k, half] = copy

        @pl.loop(0, len(dys))
        def _(q):
            dy = dys[0] + step * q + third * (q // 2) + 8
            weight_product(rows(sib_row(dy, k) * 2, 2 * S), half)
            core_copy(dy, k, half, n0 + q).start()

    def with_sibling(dy, k, half, *srcs):
        got(core[dy, k, half])
        add_rows(p, wrow(dy, k), S, HALF[half], (sib, sib_row(dy, k)), *srcs)

    def x_far(half):
        with_sibling(2, 1, half)
        far_x[half] = send(part(p, wrow(2, 1), S, half), part(xq, 0, S, half), other_h)

    def y_part(k, way, half, start, count):
        src = part(p, wrow((1, 3)[way], k) + start, count, half)
        return send(src, part(yb, yb_row(k, way) + start, count, half), ydev[way])

    def y_other(half):
        for way in WAYS:
            with_sibling((1, 3)[way], 1, half)
            near1[way, half] = y_part(1, way, half, 0, S)

    def y_near(half):
        for way in WAYS:
            with_sibling((1, 3)[way], 0, half)
            near0[way, half] = y_part(0, way, half, *CUTS[0][1 - way])

    def y_far(half):
        got(far_x[half])
        with_sibling(2, 0, half, (xq, 0))
        for way in WAYS:
            start, count = CUTS[0][way]
            src = part(p, wrow(2, 0) + start, count, half)
            far0[way, half] = send(src, part(ya, way * 80, count, half), ydev[way])

    def y_pass(half):
        for way in WAYS:
            got(far0[way, half])
            start, count = CUTS[0][way]
            to = wrow((1, 3)[way], 0) + start
            add_rows(p, to, count, HALF[half], (ya, way * 80))
            pass0[way, half] = y_part(0, way, half, start, count)

    def x_near(half):
        got(near1[0, half], near1[1, half])
        with_sibling(0, 1, half, (yb, yb_row(1, 0)), (yb, yb_row(1, 1)))
        near_x[half] = send(part(p, wrow(0, 1), S, half), part(xb, 0, S, half), other_h)

    def total_of(half):
        got(core[0, 0, half], near_x[half], *(c[way, half] for c in (near0, pass0) for way in WAYS))
        cols = pl.ds(*HALF[half])

        @pl.loop(0, S // 16)
        def _(i):
            total = xb[rows(i * 16, 16), cols].astype(F32)
            for src, start in ((p, wrow(0, 0)), (sib, sib_row(0, 0)), (yb, yb_row(0, 0)),
                               (yb, yb_row(0, 1))):
                total += src[rows(start + i * 16, 16), cols].astype(F32)
            grad_ref[rows(i * 16, 16), cols] = total

    def input_grad(l_of, pair):
        at = rows((l_of * 4 + pair % 4) * 2 * S, 2 * S)
        total = dot(w[at, 0:512], g[:, 0:512], 1, 1) + dot(w[at, 768:1408], g[:, 512:1152], 1, 1)
        ig[at, :] = total.astype(BF)

    core, far_x, near1, near0, far0, pass0, near_x = {}, {}, {}, {}, {}, {}, {}

    def za_row(k, way, step):
        return ((k * 2 + way) * 3 + step) * S

    def z_far(k):
        out = []
        for way in (0, 1):
            start, count = CUTS[k][way]
            src = ig.at[rows(arow(4, k) + start, count)]
            out.append(send(src, zh.at[rows((k * 2 + way) * 80, count)], zdev[way]))
        return out

    def z_pass(k, copies, d):
        out = []
        for way, dz in enumerate((d, 8 - d)):
            got(copies[way])
            if d == 3:
                start, count = CUTS[k][way]
                add_rows(ig, arow(dz, k) + start, count, (0, T), (zh, (k * 2 + way) * 80))
            else:
                add_rows(ig, arow(dz, k), S, (0, T), (za, za_row(k, way, 2 - d)))
            src = ig.at[rows(arow(dz, k), S)]
            out.append(send(src, za.at[rows(za_row(k, way, 3 - d), S)], zdev[way]))
        return out

    @pl.loop(0, 2)
    def _(m):
        hidden_pass(a, w, g, h, 0, m)

    weight_grads((2, 1, 3), 1, 0)
    got(*core_w[1])
    hidden_pass(a, w, g, h, 1, 0)
    x_far(0)
    y_other(0)
    hidden_pass(a, w, g, h, 1, 1)
    far_pair = ((z + 4) % 8) // 2

    @pl.loop(0, 2)
    def _(i):
        input_grad((lo + 1 + i) % 2, far_pair)

    zc = {k: z_far(k) for k in (1, 0)}
    weight_grads((2, 1, 3), 1, 1)
    weight_grads((1, 3, 2), 0, 0)
    x_far(1)
    y_other(1)

    @pl.loop(0, 4)
    def _(i):
        input_grad((lo + 1 + i // 2) % 2, far_pair + 1 + 2 * (i % 2))

    zc[1] = z_pass(1, zc[1], 3)
    y_near(0)
    y_far(0)
    zc[0] = z_pass(0, zc[0], 3)
    weight_grads((1, 3, 2), 0, 1)
    y_near(1)
    for half in (0, 1):
        for k in (1, 0):
            weight_grads((0,), k, half)

    @pl.loop(0, 2)
    def _(i):
        input_grad((lo + 1 + i) % 2, far_pair + 2)

    zc[1] = z_pass(1, zc[1], 2)
    x_near(0)
    y_far(1)
    x_near(1)
    zc[0] = z_pass(0, zc[0], 2)
    y_pass(0)
    zc[1] = z_pass(1, zc[1], 1)
    y_pass(1)
    zc[0] = z_pass(0, zc[0], 1)
    got(*zc[1])
    add_rows(ig, arow(0, 1), S, (0, T), (za, za_row(1, 0, 2)), (za, za_row(1, 1, 2)))
    z_x = send(ig.at[rows(arow(0, 1), S)], xl, other_l)
    total_of(0)

    got(*zc[0], z_x)
    total = ig[rows(arow(0, 0), S), :].astype(F32) + xl[...].astype(F32)
    for way in (0, 1):
        total += za[rows(za_row(0, way, 2), S), :].astype(F32)
    ig_ref[...] = total
    total_of(1)
    drain()


def moments(m, v, grad):
    m_new = 0.9 * m + 0.1 * grad
    v_new = 0.95 * v + 0.05 * grad * grad
    return m_new, v_new, m_new / (jnp.sqrt(v_new) + 1e-8)


def finish(dp_ref, grad_hbm, ig_hbm, mask_hbm, mgu_hbm, vgu_hbm, md_hbm, vd_hbm,
           out_hbm, mgu_new, vgu_new, sgu_new, md_new, vd_new, sd_new,
           grad_ref, ig_ref, mask, out, old, new, in_sem, out_sem):
    firsts = (mgu_hbm.at[0], mgu_hbm.at[1], md_hbm)
    seconds = (vgu_hbm.at[0], vgu_hbm.at[1], vd_hbm)
    loads = [
        pltpu.make_async_copy(mask_hbm, mask, in_sem.at[6]),
        pltpu.make_async_copy(grad_hbm, grad_ref, in_sem.at[7]),
        pltpu.make_async_copy(ig_hbm, ig_ref, in_sem.at[8]),
    ]
    for k in range(3):
        loads.append(pltpu.make_async_copy(firsts[k], old.at[2 * k], in_sem.at[2 * k]))
        loads.append(pltpu.make_async_copy(seconds[k], old.at[2 * k + 1], in_sem.at[2 * k + 1]))
    for load in loads:
        load.start()
    loads[2].wait()
    out[...] = ig_ref[...].astype(BF)
    stores = [pltpu.make_async_copy(out, out_hbm, out_sem.at[9])]
    stores[0].start()
    loads[0].wait()
    loads[1].wait()
    scale = jnp.float32(8192.0) ** -0.5
    keep = jnp.where(keep_of(mask, dp_ref[0]) != 0, scale, 0.0)
    rest = grad_ref[:, 1280:1408]
    lanes = ((0, 768), (256, 1024), (512, 1408))
    results = ((mgu_new.at[0], vgu_new.at[0], sgu_new.at[0]),
               (mgu_new.at[1], vgu_new.at[1], sgu_new.at[1]),
               (md_new, vd_new, sd_new))
    for k in range(3):
        tail = (rest, pltpu.roll(rest, 64, 1), grad_ref[:, 1664:PK])[k][:, : F - MAIN]
        parts = [grad_ref[:, n : n + 256] for n in lanes[k]]
        grad = jnp.concatenate([*parts, tail], 1)
        loads[3 + 2 * k].wait()
        loads[4 + 2 * k].wait()
        new[3 * k], new[3 * k + 1], new[3 * k + 2] = moments(
            old[2 * k], old[2 * k + 1], grad * keep
        )
        for n in range(3):
            store = pltpu.make_async_copy(new.at[3 * k + n], results[k][n], out_sem.at[3 * k + n])
            store.start()
            stores.append(store)
    for store in stores:
        store.wait()


VMEM = pl.BlockSpec(memory_space=pltpu.VMEM)
HBM = pl.BlockSpec(memory_space=pltpu.HBM)
sds = jax.ShapeDtypeStruct


def ffn(tokens, cotangent, mask, wgu, wd):
    return pl.pallas_call(
        body,
        name="ffn_grads",
        out_shape=(sds((S, PK), F32), sds((S, T), F32)),
        in_specs=[HBM] * 5,
        out_specs=(VMEM, VMEM),
        scratch_shapes=[
            pltpu.VMEM(mask.shape, jnp.int32),
            pltpu.VMEM(wgu.shape, BF),
            pltpu.VMEM(wd.shape, BF),
            pltpu.SemaphoreType.DMA((5,)),
            pltpu.VMEM((D, 2 * T), BF),
            pltpu.VMEM((D, PK), BF),
            pltpu.VMEM((D, PK), BF),
            pltpu.VMEM((T, 1152), BF),
            pltpu.VMEM((T, 640), BF),
            pltpu.VMEM((D, T), BF),
            pltpu.VMEM((8 * S, PK), BF),
            pltpu.VMEM((2 * 80, PK), BF),
            pltpu.VMEM((4 * S, PK), BF),
            pltpu.VMEM((S, PK), BF),
            pltpu.VMEM((S, PK), BF),
            pltpu.VMEM((12 * S, T), BF),
            pltpu.VMEM((4 * 80, T), BF),
            pltpu.VMEM((S, T), BF),
            pltpu.SemaphoreType.DMA((COPIES,)),
            pltpu.SemaphoreType.DMA((COPIES,)),
        ],
        compiler_params=pltpu.CompilerParams(
            collective_id=0, has_side_effects=True, vmem_limit_bytes=62 << 20
        ),
    )(tokens, cotangent, mask, wgu, wd)


def on_device(tokens, cotangent, mask, wgu, wd, mgu, vgu, md, vd):
    grad, ig = ffn(tokens.T, cotangent.T, mask, wgu, wd.T)
    dp = lax.axis_index("dp").astype(jnp.int32).reshape(1)
    big, down = sds((2, S, F), F32), sds((S, F), F32)
    out = pl.pallas_call(
        finish,
        name="moments",
        out_shape=(sds((S, T), BF), big, big, big, down, down, down),
        in_specs=[pl.BlockSpec(memory_space=pltpu.SMEM)] + [HBM] * 7,
        out_specs=(HBM,) * 7,
        scratch_shapes=[
            pltpu.VMEM((S, PK), F32),
            pltpu.VMEM((S, T), F32),
            pltpu.VMEM(mask.shape, jnp.int32),
            pltpu.VMEM((S, T), BF),
            pltpu.VMEM((6, S, F), F32),
            pltpu.VMEM((9, S, F), F32),
            pltpu.SemaphoreType.DMA((9,)),
            pltpu.SemaphoreType.DMA((10,)),
        ],
        compiler_params=pltpu.CompilerParams(vmem_limit_bytes=62 << 20),
    )(dp, grad, ig, mask, mgu, vgu, md.T, vd.T)
    return (out[0].T, *out[1:4], *(x.T for x in out[4:]))


def solution(mesh):
    return jax.shard_map(
        on_device,
        mesh=mesh,
        in_specs=(
            P("dp", "tensor"),
            P("dp", "tensor"),
            P(None, "tensor"),
            P(None, "dp", "tensor"),
            P("tensor", "dp"),
            P(None, "dp", "tensor"),
            P(None, "dp", "tensor"),
            P("tensor", "dp"),
            P("tensor", "dp"),
        ),
        out_specs=(
            P("dp", "tensor"),
            P(None, "dp", "tensor"),
            P(None, "dp", "tensor"),
            P(None, "dp", "tensor"),
            P("tensor", "dp"),
            P("tensor", "dp"),
            P("tensor", "dp"),
        ),
        check_vma=False,
    )
```

```python
import functools
import jax
import jax.numpy as jnp
from jax import lax
from jax.experimental import pallas as pl
from jax.experimental.pallas import tpu as pltpu
from jax.sharding import PartitionSpec as P

BF = jnp.bfloat16
F32 = jnp.float32
MESH = pl.DeviceIdType.MESH

D = 2304
S = 144
T = 512
F = 576
MAIN = 512
PK = 1792
HALF = ((0, 768), (768, 1024))
GLANES = ((0, 512), (512, 640))
HLANES = ((0, 256), (256, 384))
CUTS = (((0, 80), (80, 64)), ((80, 64), (0, 80)))
WAYS = (0, 1)
COPIES = 128


def dot(a, b, ca, cb):
    return lax.dot_general(a, b, (((ca,), (cb,)), ((), ())), preferred_element_type=F32)


def rows(start, count, step=16):
    return pl.ds(pl.multiple_of(start, step), count)


def keep_of(mask_ref, dp):
    block = dp + dp // 8
    first = 128 - 16 * (dp % 8)
    row = lax.broadcasted_iota(jnp.int32, (S, F), 0)
    return jnp.where(row < first, mask_ref[pl.ds(block, 1), :], mask_ref[pl.ds(block + 1, 1), :])


def pack(ref, at, keep, gate, up, down):
    gate, up, down = (jnp.where(keep != 0, w.astype(F32), 0.0) for w in (gate, up, down))
    at_lane = 0
    rest = jnp.concatenate([gate[:, MAIN:], up[:, MAIN:]], 1)
    last = jnp.concatenate([down[:, MAIN:], jnp.zeros_like(down[:, MAIN:])], 1)
    for part in (gate[:, :256], up[:, :256], down[:, :256], gate[:, 256:MAIN], up[:, 256:MAIN],
                 rest, down[:, 256:MAIN], last):
        ref[at, at_lane : at_lane + part.shape[1]] = part.astype(BF)
        at_lane += part.shape[1]


def add_rows(dst, to, n, lanes, *srcs):
    cols = pl.ds(*lanes)

    @pl.loop(0, n // 16)
    def _(i):
        at = rows(to + i * 16, 16)
        total = dst[at, cols].astype(F32)
        for src, start in srcs:
            total += src[rows(start + i * 16, 16), cols].astype(F32)
        dst[at, cols] = total.astype(dst.dtype)


def grads_of(gate, up, hidden_grad):
    sig = jax.nn.sigmoid(gate)
    silu = gate * sig
    gate_grad = hidden_grad * up * (sig * (1.0 + gate * (1.0 - sig)))
    return gate_grad, hidden_grad * silu, silu * up


def hidden_pass(a, w, g, h, half, m):
    tok, mine = rows(m * 256, 256, 256), rows(m * D, D, D)
    first, (gl, gn), (hl, hn) = HALF[half][0], GLANES[half], HLANES[half]
    both = dot(a[mine, 0:256], w[:, first : first + gn], 0, 0)
    hg = dot(a[mine, 256:512], w[:, first + gn : first + gn + hn], 0, 0)
    gate_grad, up_grad, hidden = grads_of(both[:, :256], both[:, 256:512], hg[:, :256])
    g[tok, gl : gl + 256] = gate_grad.astype(BF)
    g[tok, gl + 256 : gl + 512] = up_grad.astype(BF)
    h[tok, hl : hl + 256] = hidden.astype(BF)
    if half == 1:
        both, hg = both[:, 512:], hg[:, 256:]
        gate_grad, up_grad, hidden = grads_of(both, pltpu.roll(both, 64, 1), hg)
        low = lax.broadcasted_iota(jnp.int32, (256, 128), 1) < 64
        g[tok, 1024:1152] = jnp.where(low, gate_grad, pltpu.roll(up_grad, 64, 1)).astype(BF)
        h[tok, 512:640] = jnp.where(low, hidden, 0.0).astype(BF)


def body(tok_hbm, cot_hbm, mask_hbm, wgu_hbm, wd_hbm, grad_ref, ig_ref,
         mask_ref, wgu_ref, wd_ref, in_sem, a, w, p, g, h, ig, sib, ya, yb, xb, xq, za, zh, xl, send_sem, recv_sem):
    dp, tensor = lax.axis_index("dp"), lax.axis_index("tensor")
    y, hi, c = dp // 4, (dp // 2) % 2, dp % 2
    lo, z = tensor // 8, tensor % 8
    hk = (hi, 1 - hi)
    lk = (lo, 1 - lo)

    def dp_at(dy, k, flip=0):
        return (((y + dy) % 4) * 2 + hk[k]) * 2 + (1 - c if flip else c)

    def t_at(dz, k):
        return lk[k] * 8 + (z + dz) % 8

    up_y, down_y = (dp_at(1, 0), tensor), (dp_at(3, 0), tensor)
    up_z, down_z = (dp, t_at(1, 0)), (dp, t_at(7, 0))
    other_h, other_l, sibling = (dp_at(0, 1), tensor), (dp, t_at(0, 1)), (dp_at(0, 0, 1), tensor)
    ydev, zdev = (up_y, down_y), (up_z, down_z)

    moves = [(mask_hbm, mask_ref), (wgu_hbm, wgu_ref), (wd_hbm, wd_ref)]
    for m in (0, 1):
        own = rows((lo * 8 + z) * S + m * D, S)
        for n, src in enumerate((tok_hbm, cot_hbm)):
            moves.append((src.at[:, pl.ds(m * 256, 256)], a.at[own, pl.ds(n * 256, 256)]))
    loads = [pltpu.make_async_copy(*move, in_sem.at[n]) for n, move in enumerate(moves)]
    for load in loads:
        load.start()

    barrier = pltpu.get_barrier_semaphore()
    partners = (up_y, down_y, up_z, down_z, other_h, other_l, sibling)
    for dev in partners:
        pl.semaphore_signal(barrier, inc=1, device_id=dev, device_id_type=MESH)

    sent = []

    def send(src, dst, dev):
        n = len(sent)
        copy = pltpu.make_async_remote_copy(
            src, dst, send_sem.at[n], recv_sem.at[n], device_id=dev, device_id_type=MESH
        )
        copy.start()
        sent.append(copy)
        return copy

    def drain():
        for copy in sent:
            copy.wait_send()

    def got(*copies):
        for copy in copies:
            copy.wait_recv()

    def same(ref, start, count, dev):
        part = ref.at[rows(start, count)]
        return send(part, part, dev)

    def wrow(dy, k, flip=0):
        return dp_at(dy, k, flip) * S

    def arow(dz, k):
        return t_at(dz, k) * S

    def part(ref, start, count, half):
        return ref.at[rows(start, count), pl.ds(*HALF[half])]

    def part_of(ref, start, part, dev):
        return same(ref, start + part * D, S, dev)

    def to_sibling(dy, k):
        w_c.append(same(w, wrow(dy, k), S, sibling))

    for load in loads:
        load.wait()
    pack(w, rows(wrow(0, 0), S), keep_of(mask_ref, dp), wgu_ref[0], wgu_ref[1], wd_ref[...])
    pl.semaphore_wait(barrier, len(partners))
    core_w, a_l = ([], []), ([], [])
    a0, a1, a2, a3, b0, b1, a_x = {}, {}, {}, {}, {}, {}, {}
    w0, w1, v0, v1, w_x = {}, {}, {}, {}, {}

    def w_send(start, count, half, dev):
        src = part(w, start, count, half)
        return send(src, src, dev)

    def to_sibling(dy, k, half):
        core_w[half].append(w_send(wrow(dy, k), S, half, sibling))

    def w_start(out, k, half):
        for way in WAYS:
            out[way, half] = w_send(wrow(0, k), S, half, ydev[way])

    def w_next(copies, out, k, half):
        for way in WAYS:
            got(copies[way, half])
            start, count = CUTS[k][way]
            out[way, half] = w_send(wrow((3, 1)[way], k) + start, count, half, ydev[way])
            to_sibling((3, 1)[way], k, half)

    def w_last(copies, k, half):
        got(copies[0, half], copies[1, half])
        to_sibling(2, k, half)

    def a_next(copies, out, k, d, part, way):
        got(copies[way, part])
        out[way, part] = part_of(a, arow((8 - d, d)[way], k), part, zdev[way])

    def a_start(out, k, part):
        for way in WAYS:
            out[way, part] = part_of(a, arow(0, k), part, zdev[way])

    def a_both(copies, out, k, d, part):
        for way in WAYS:
            a_next(copies, out, k, d, part, way)

    def a_over(dz, part):
        a_l[part].append(part_of(a, arow(dz, 0), part, other_l))

    def a_third(part):
        for way in WAYS:
            if way == part:
                a_next(a2, a3, 0, 3, part, way)
            else:
                got(a2[way, part])
            a_over((5, 3)[way], part)

    def a_fourth(part):
        got(a3[part, part])
        a_over(4, part)

    for n in (0, 1):
        a_x[n] = part_of(a, arow(0, 0), n, other_l)
        a_start(a0, 0, n)
        w_start(w0, 0, n)
        w_x[n] = w_send(wrow(0, 0), S, n, other_h)
    for half in (0, 1):
        to_sibling(0, 0, half)
    a_both(a0, a1, 0, 1, 0)
    w_next(w0, w1, 0, 0)
    a_both(a0, a1, 0, 1, 1)
    a_both(a1, a2, 0, 2, 0)
    got(a_x[0])
    a_start(b0, 1, 0)
    w_next(w0, w1, 0, 1)
    got(w_x[0])
    w_start(v0, 1, 0)
    to_sibling(0, 1, 0)
    a_both(a1, a2, 0, 2, 1)
    got(a_x[1])
    a_start(b0, 1, 1)
    a_third(0)
    got(w_x[1])
    w_start(v0, 1, 1)
    to_sibling(0, 1, 1)
    w_last(w1, 0, 0)
    a_both(b0, b1, 1, 1, 0)
    a_third(1)
    a_fourth(0)
    w_last(w1, 0, 1)
    w_next(v0, v1, 1, 0)
    a_both(b0, b1, 1, 1, 1)
    a_fourth(1)
    w_next(v0, v1, 1, 1)
    w_last(v1, 1, 0)
    got(b1[0, 0], b1[1, 0], *a_l[0], *core_w[0])
    hidden_pass(a, w, g, h, 0, 0)
    w_last(v1, 1, 1)
    got(b1[0, 1], b1[1, 1], *a_l[1])
    hidden_pass(a, w, g, h, 0, 1)

    def sib_row(dy, k):
        return (dp_at(dy, k) // 2) * S

    def yb_row(k, way):
        return (k * 2 + way) * S

    def weight_product(start, half):
        at = rows(start, 2 * S)
        ats = [rows(start + m * D, 2 * S) for m in (0, 1)]
        toks = (slice(0, 256), slice(256, 512))
        first, (gl, gn), (hl, hn) = HALF[half][0], GLANES[half], HLANES[half]
        total = sum(dot(a[r, 0:256], g[t, gl : gl + gn], 1, 0) for r, t in zip(ats, toks))
        p[at, first : first + gn] = total.astype(BF)
        total = sum(dot(a[r, 256:512], h[t, hl : hl + hn], 1, 0) for r, t in zip(ats, toks))
        p[at, first + gn : first + gn + hn] = total.astype(BF)

    def core_copy(dy, k, half, n):
        return pltpu.make_async_remote_copy(
            part(p, wrow(dy, k, 1), S, half), part(sib, sib_row(dy, k), S, half),
            send_sem.at[n], recv_sem.at[n], device_id=sibling, device_id_type=MESH,
        )

    def weight_grads(dys, k, half):
        n0 = len(sent)
        step = (dys[1] - dys[0]) % 4 if len(dys) > 1 else 0
        third = dys[2] - dys[0] - 2 * step if len(dys) > 2 else 0
        for q, dy in enumerate(dys):
            copy = core_copy(dy, k, half, n0 + q)
            sent.append(copy)
            core[dy, k, half] = copy

        @pl.loop(0, len(dys))
        def _(q):
            dy = dys[0] + step * q + third * (q // 2) + 8
            weight_product(sib_row(dy, k) * 2, half)
            core_copy(dy, k, half, n0 + q).start()

    def with_sibling(dy, k, half, *srcs):
        got(core[dy, k, half])
        add_rows(p, wrow(dy, k), S, HALF[half], (sib, sib_row(dy, k)), *srcs)

    def x_far(half):
        with_sibling(2, 1, half)
        far_x[half] = send(part(p, wrow(2, 1), S, half), part(xq, 0, S, half), other_h)

    def y_part(k, way, half, start, count):
        src = part(p, wrow((1, 3)[way], k) + start, count, half)
        return send(src, part(yb, yb_row(k, way) + start, count, half), ydev[way])

    def y_other(half):
        for way in WAYS:
            with_sibling((1, 3)[way], 1, half)
            near1[way, half] = y_part(1, way, half, 0, S)

    def y_near(half):
        for way in WAYS:
            with_sibling((1, 3)[way], 0, half)
            near0[way, half] = y_part(0, way, half, *CUTS[half][1 - way])

    def y_far(half):
        got(far_x[half])
        with_sibling(2, 0, half, (xq, 0))
        for way in WAYS:
            start, count = CUTS[half][way]
            src = part(p, wrow(2, 0) + start, count, half)
            far0[way, half] = send(src, part(ya, way * 80, count, half), ydev[way])

    def y_pass(half):
        for way in WAYS:
            got(far0[way, half])
            start, count = CUTS[half][way]
            to = wrow((1, 3)[way], 0) + start
            add_rows(p, to, count, HALF[half], (ya, way * 80))
            pass0[way, half] = y_part(0, way, half, start, count)

    def x_near(half):
        got(near1[0, half], near1[1, half])
        with_sibling(0, 1, half, (yb, yb_row(1, 0)), (yb, yb_row(1, 1)))
        near_x[half] = send(part(p, wrow(0, 1), S, half), part(xb, 0, S, half), other_h)

    def total_of(half):
        got(core[0, 0, half], near_x[half], *(c[way, half] for c in (near0, pass0) for way in WAYS))
        cols = pl.ds(*HALF[half])

        @pl.loop(0, S // 16)
        def _(i):
            total = xb[rows(i * 16, 16), cols].astype(F32)
            for src, start in ((p, wrow(0, 0)), (sib, sib_row(0, 0)), (yb, yb_row(0, 0)),
                               (yb, yb_row(0, 1))):
                total += src[rows(start + i * 16, 16), cols].astype(F32)
            grad_ref[rows(i * 16, 16), cols] = total

    def input_grad(l_of, pair):
        at = rows((l_of * 4 + pair % 4) * 2 * S, 2 * S)
        total = dot(w[at, 0:512], g[:, 0:512], 1, 1) + dot(w[at, 768:1408], g[:, 512:1152], 1, 1)
        ig[at, :] = total.astype(BF)

    core, far_x, near1, near0, far0, pass0, near_x = {}, {}, {}, {}, {}, {}, {}

    def za_row(k, way, step):
        return ((k * 2 + way) * 3 + step) * S

    def z_far(k):
        out = []
        for way in (0, 1):
            start, count = CUTS[k][way]
            src = ig.at[rows(arow(4, k) + start, count)]
            out.append(send(src, zh.at[rows((k * 2 + way) * 80, count)], zdev[way]))
        return out

    def z_pass(k, copies, d):
        out = []
        for way, dz in enumerate((d, 8 - d)):
            got(copies[way])
            if d == 3:
                start, count = CUTS[k][way]
                add_rows(ig, arow(dz, k) + start, count, (0, T), (zh, (k * 2 + way) * 80))
            else:
                add_rows(ig, arow(dz, k), S, (0, T), (za, za_row(k, way, 2 - d)))
            src = ig.at[rows(arow(dz, k), S)]
            out.append(send(src, za.at[rows(za_row(k, way, 3 - d), S)], zdev[way]))
        return out

    weight_grads((2, 1, 3), 1, 0)
    got(*core_w[1])
    hidden_pass(a, w, g, h, 1, 0)
    x_far(0)
    y_other(0)
    hidden_pass(a, w, g, h, 1, 1)
    far_pair = ((z + 4) % 8) // 2
    zc = {}

    def beside(k):
        @pl.loop(0, 2)
        def _(i):
            input_grad(lk[k], far_pair + 1 + 2 * i)

        zc[k] = z_pass(k, zc[k], 3)

    input_grad(lk[1], far_pair)
    zc[1] = z_far(1)
    weight_grads((2, 1, 3), 1, 1)
    input_grad(lk[0], far_pair)
    zc[0] = z_far(0)
    x_far(1)
    y_other(1)
    beside(1)
    weight_grads((2, 1, 3), 0, 0)
    beside(0)
    y_far(0)
    y_near(0)
    weight_grads((2, 1, 3), 0, 1)
    for half in (0, 1):
        weight_grads((0,), 1, half)
    zc[1] = z_pass(1, zc[1], 2)
    for half in (0, 1):
        weight_grads((0,), 0, half)
    x_near(0)
    y_far(1)
    y_near(1)
    x_near(1)

    @pl.loop(0, 2)
    def _(i):
        input_grad((lo + 1 + i) % 2, far_pair + 2)

    zc[0] = z_pass(0, zc[0], 2)
    y_pass(0)
    zc[1] = z_pass(1, zc[1], 1)
    zc[0] = z_pass(0, zc[0], 1)
    y_pass(1)
    got(*zc[1])
    add_rows(ig, arow(0, 1), S, (0, T), (za, za_row(1, 0, 2)), (za, za_row(1, 1, 2)))
    z_x = send(ig.at[rows(arow(0, 1), S)], xl, other_l)
    total_of(0)

    got(*zc[0], z_x)
    total = ig[rows(arow(0, 0), S), :].astype(F32) + xl[...].astype(F32)
    for way in (0, 1):
        total += za[rows(za_row(0, way, 2), S), :].astype(F32)
    ig_ref[...] = total
    total_of(1)
    drain()


def moments(m, v, grad):
    m_new = 0.9 * m + 0.1 * grad
    v_new = 0.95 * v + 0.05 * grad * grad
    return m_new, v_new, m_new / (jnp.sqrt(v_new) + 1e-8)


def finish(dp_ref, grad_hbm, ig_hbm, mask_hbm, mgu_hbm, vgu_hbm, md_hbm, vd_hbm,
           out_hbm, mgu_new, vgu_new, sgu_new, md_new, vd_new, sd_new,
           grad_ref, ig_ref, mask, out, old, new, in_sem, out_sem):
    firsts = (mgu_hbm.at[0], mgu_hbm.at[1], md_hbm)
    seconds = (vgu_hbm.at[0], vgu_hbm.at[1], vd_hbm)
    loads = [
        pltpu.make_async_copy(mask_hbm, mask, in_sem.at[6]),
        pltpu.make_async_copy(grad_hbm, grad_ref, in_sem.at[7]),
        pltpu.make_async_copy(ig_hbm, ig_ref, in_sem.at[8]),
    ]
    for k in range(3):
        loads.append(pltpu.make_async_copy(firsts[k], old.at[2 * k], in_sem.at[2 * k]))
        loads.append(pltpu.make_async_copy(seconds[k], old.at[2 * k + 1], in_sem.at[2 * k + 1]))
    for load in loads:
        load.start()
    loads[2].wait()
    out[...] = ig_ref[...].astype(BF)
    stores = [pltpu.make_async_copy(out, out_hbm, out_sem.at[9])]
    stores[0].start()
    loads[0].wait()
    loads[1].wait()
    scale = jnp.float32(8192.0) ** -0.5
    keep = jnp.where(keep_of(mask, dp_ref[0]) != 0, scale, 0.0)
    rest = grad_ref[:, 1280:1408]
    lanes = ((0, 768), (256, 1024), (512, 1408))
    results = ((mgu_new.at[0], vgu_new.at[0], sgu_new.at[0]),
               (mgu_new.at[1], vgu_new.at[1], sgu_new.at[1]),
               (md_new, vd_new, sd_new))
    for k in range(3):
        tail = (rest, pltpu.roll(rest, 64, 1), grad_ref[:, 1664:PK])[k][:, : F - MAIN]
        parts = [grad_ref[:, n : n + 256] for n in lanes[k]]
        grad = jnp.concatenate([*parts, tail], 1)
        loads[3 + 2 * k].wait()
        loads[4 + 2 * k].wait()
        new[3 * k], new[3 * k + 1], new[3 * k + 2] = moments(
            old[2 * k], old[2 * k + 1], grad * keep
        )
        for n in range(3):
            store = pltpu.make_async_copy(new.at[3 * k + n], results[k][n], out_sem.at[3 * k + n])
            store.start()
            stores.append(store)
    for store in stores:
        store.wait()


VMEM = pl.BlockSpec(memory_space=pltpu.VMEM)
HBM = pl.BlockSpec(memory_space=pltpu.HBM)
sds = jax.ShapeDtypeStruct


def ffn(tokens, cotangent, mask, wgu, wd):
    return pl.pallas_call(
        body,
        name="ffn_grads",
        out_shape=(sds((S, PK), F32), sds((S, T), F32)),
        in_specs=[HBM] * 5,
        out_specs=(VMEM, VMEM),
        scratch_shapes=[
            pltpu.VMEM(mask.shape, jnp.int32),
            pltpu.VMEM(wgu.shape, BF),
            pltpu.VMEM(wd.shape, BF),
            pltpu.SemaphoreType.DMA((7,)),
            pltpu.VMEM((2 * D, T), BF),
            pltpu.VMEM((D, PK), BF),
            pltpu.VMEM((D, PK), BF),
            pltpu.VMEM((T, 1152), BF),
            pltpu.VMEM((T, 640), BF),
            pltpu.VMEM((D, T), BF),
            pltpu.VMEM((8 * S, PK), BF),
            pltpu.VMEM((2 * 80, PK), BF),
            pltpu.VMEM((4 * S, PK), BF),
            pltpu.VMEM((S, PK), BF),
            pltpu.VMEM((S, PK), BF),
            pltpu.VMEM((12 * S, T), BF),
            pltpu.VMEM((4 * 80, T), BF),
            pltpu.VMEM((S, T), BF),
            pltpu.SemaphoreType.DMA((COPIES,)),
            pltpu.SemaphoreType.DMA((COPIES,)),
        ],
        compiler_params=pltpu.CompilerParams(
            collective_id=0, has_side_effects=True, vmem_limit_bytes=62 << 20
        ),
    )(tokens, cotangent, mask, wgu, wd)


def on_device(tokens, cotangent, mask, wgu, wd, mgu, vgu, md, vd):
    grad, ig = ffn(tokens.T, cotangent.T, mask, wgu, wd.T)
    dp = lax.axis_index("dp").astype(jnp.int32).reshape(1)
    big, down = sds((2, S, F), F32), sds((S, F), F32)
    out = pl.pallas_call(
        finish,
        name="moments",
        out_shape=(sds((S, T), BF), big, big, big, down, down, down),
        in_specs=[pl.BlockSpec(memory_space=pltpu.SMEM)] + [HBM] * 7,
        out_specs=(HBM,) * 7,
        scratch_shapes=[
            pltpu.VMEM((S, PK), F32),
            pltpu.VMEM((S, T), F32),
            pltpu.VMEM(mask.shape, jnp.int32),
            pltpu.VMEM((S, T), BF),
            pltpu.VMEM((6, S, F), F32),
            pltpu.VMEM((9, S, F), F32),
            pltpu.SemaphoreType.DMA((9,)),
            pltpu.SemaphoreType.DMA((10,)),
        ],
        compiler_params=pltpu.CompilerParams(vmem_limit_bytes=62 << 20),
    )(dp, grad, ig, mask, mgu, vgu, md.T, vd.T)
    return (out[0].T, *out[1:4], *(x.T for x in out[4:]))


def solution(mesh):
    return jax.shard_map(
        on_device,
        mesh=mesh,
        in_specs=(
            P("dp", "tensor"),
            P("dp", "tensor"),
            P(None, "tensor"),
            P(None, "dp", "tensor"),
            P("tensor", "dp"),
            P(None, "dp", "tensor"),
            P(None, "dp", "tensor"),
            P("tensor", "dp"),
            P("tensor", "dp"),
        ),
        out_specs=(
            P("dp", "tensor"),
            P(None, "dp", "tensor"),
            P(None, "dp", "tensor"),
            P(None, "dp", "tensor"),
            P("tensor", "dp"),
            P("tensor", "dp"),
            P("tensor", "dp"),
        ),
        check_vma=False,
    )
```

```python
import functools
import jax
import jax.numpy as jnp
from jax import lax
from jax.experimental import pallas as pl
from jax.experimental.pallas import tpu as pltpu
from jax.sharding import PartitionSpec as P

BF = jnp.bfloat16
F32 = jnp.float32
MESH = pl.DeviceIdType.MESH

D = 2304
S = 144
T = 512
F = 576
MAIN = 512
PK = 1792
HALF = ((0, 768), (768, 1024))
GLANES = ((0, 512), (512, 640))
HLANES = ((0, 256), (256, 384))
CUTS = (((0, 80), (80, 64)), ((80, 64), (0, 80)))
WAYS = (0, 1)
COPIES = 128


def dot(a, b, ca, cb):
    return lax.dot_general(a, b, (((ca,), (cb,)), ((), ())), preferred_element_type=F32)


def rows(start, count, step=16):
    return pl.ds(pl.multiple_of(start, step), count)


def keep_of(mask_ref, dp):
    block = dp + dp // 8
    first = 128 - 16 * (dp % 8)
    row = lax.broadcasted_iota(jnp.int32, (S, F), 0)
    return jnp.where(row < first, mask_ref[pl.ds(block, 1), :], mask_ref[pl.ds(block + 1, 1), :])


def pack(ref, at, keep, gate, up, down):
    gate, up, down = (jnp.where(keep != 0, w.astype(F32), 0.0) for w in (gate, up, down))
    at_lane = 0
    rest = jnp.concatenate([gate[:, MAIN:], up[:, MAIN:]], 1)
    last = jnp.concatenate([down[:, MAIN:], jnp.zeros_like(down[:, MAIN:])], 1)
    for part in (gate[:, :256], up[:, :256], down[:, :256], gate[:, 256:MAIN], up[:, 256:MAIN],
                 rest, down[:, 256:MAIN], last):
        ref[at, at_lane : at_lane + part.shape[1]] = part.astype(BF)
        at_lane += part.shape[1]


def add_rows(dst, to, n, lanes, *srcs):
    cols = pl.ds(*lanes)

    @pl.loop(0, n // 16)
    def _(i):
        at = rows(to + i * 16, 16)
        total = dst[at, cols].astype(F32)
        for src, start in srcs:
            total += src[rows(start + i * 16, 16), cols].astype(F32)
        dst[at, cols] = total.astype(dst.dtype)


def grads_of(gate, up, hidden_grad):
    sig = jax.nn.sigmoid(gate)
    silu = gate * sig
    gate_grad = hidden_grad * up * (sig * (1.0 + gate * (1.0 - sig)))
    return gate_grad, hidden_grad * silu, silu * up


def hidden_pass(a, w, g, h, half, m):
    tok, mine = rows(m * 256, 256, 256), rows(m * D, D, D)
    first, (gl, gn), (hl, hn) = HALF[half][0], GLANES[half], HLANES[half]
    both = dot(a[mine, 0:256], w[:, first : first + gn], 0, 0)
    hg = dot(a[mine, 256:512], w[:, first + gn : first + gn + hn], 0, 0)
    gate_grad, up_grad, hidden = grads_of(both[:, :256], both[:, 256:512], hg[:, :256])
    g[tok, gl : gl + 256] = gate_grad.astype(BF)
    g[tok, gl + 256 : gl + 512] = up_grad.astype(BF)
    h[tok, hl : hl + 256] = hidden.astype(BF)
    if half == 1:
        both, hg = both[:, 512:], hg[:, 256:]
        gate_grad, up_grad, hidden = grads_of(both, pltpu.roll(both, 64, 1), hg)
        low = lax.broadcasted_iota(jnp.int32, (256, 128), 1) < 64
        g[tok, 1024:1152] = jnp.where(low, gate_grad, pltpu.roll(up_grad, 64, 1)).astype(BF)
        h[tok, 512:640] = jnp.where(low, hidden, 0.0).astype(BF)


def body(tok_hbm, cot_hbm, mask_hbm, wgu_hbm, wd_hbm, grad_hbm, ig_hbm,
         grad_ref, ig_ref, out_sem, mask_ref, wgu_ref, wd_ref, in_sem, a, w, p, g, h, ig, sib, ya, yb, xb, xq, za, zh, xl, send_sem, recv_sem):
    dp, tensor = lax.axis_index("dp"), lax.axis_index("tensor")
    y, hi, c = dp // 4, (dp // 2) % 2, dp % 2
    lo, z = tensor // 8, tensor % 8
    hk = (hi, 1 - hi)
    lk = (lo, 1 - lo)

    def dp_at(dy, k, flip=0):
        return (((y + dy) % 4) * 2 + hk[k]) * 2 + (1 - c if flip else c)

    def t_at(dz, k):
        return lk[k] * 8 + (z + dz) % 8

    up_y, down_y = (dp_at(1, 0), tensor), (dp_at(3, 0), tensor)
    up_z, down_z = (dp, t_at(1, 0)), (dp, t_at(7, 0))
    other_h, other_l, sibling = (dp_at(0, 1), tensor), (dp, t_at(0, 1)), (dp_at(0, 0, 1), tensor)
    ydev, zdev = (up_y, down_y), (up_z, down_z)

    moves = [(mask_hbm, mask_ref), (wgu_hbm, wgu_ref), (wd_hbm, wd_ref)]
    for m in (0, 1):
        own = rows((lo * 8 + z) * S + m * D, S)
        for n, src in enumerate((tok_hbm, cot_hbm)):
            moves.append((src.at[:, pl.ds(m * 256, 256)], a.at[own, pl.ds(n * 256, 256)]))
    loads = [pltpu.make_async_copy(*move, in_sem.at[n]) for n, move in enumerate(moves)]
    for load in loads:
        load.start()

    barrier = pltpu.get_barrier_semaphore()
    partners = (up_y, down_y, up_z, down_z, other_h, other_l, sibling)
    for dev in partners:
        pl.semaphore_signal(barrier, inc=1, device_id=dev, device_id_type=MESH)

    sent = []

    def send(src, dst, dev):
        n = len(sent)
        copy = pltpu.make_async_remote_copy(
            src, dst, send_sem.at[n], recv_sem.at[n], device_id=dev, device_id_type=MESH
        )
        copy.start()
        sent.append(copy)
        return copy

    def drain():
        for copy in sent:
            copy.wait_send()

    def got(*copies):
        for copy in copies:
            copy.wait_recv()

    def same(ref, start, count, dev):
        part = ref.at[rows(start, count)]
        return send(part, part, dev)

    def wrow(dy, k, flip=0):
        return dp_at(dy, k, flip) * S

    def arow(dz, k):
        return t_at(dz, k) * S

    def part(ref, start, count, half):
        return ref.at[rows(start, count), pl.ds(*HALF[half])]

    def part_of(ref, start, part, dev):
        return same(ref, start + part * D, S, dev)

    def to_sibling(dy, k):
        w_c.append(same(w, wrow(dy, k), S, sibling))

    for load in loads:
        load.wait()
    pack(w, rows(wrow(0, 0), S), keep_of(mask_ref, dp), wgu_ref[0], wgu_ref[1], wd_ref[...])
    pl.semaphore_wait(barrier, len(partners))
    core_w, a_l = ([], []), ([], [])
    a0, a1, a2, a3, b0, b1, a_x = {}, {}, {}, {}, {}, {}, {}
    w0, w1, v0, v1, w_x = {}, {}, {}, {}, {}

    def w_send(start, count, half, dev):
        src = part(w, start, count, half)
        return send(src, src, dev)

    def to_sibling(dy, k, half):
        core_w[half].append(w_send(wrow(dy, k), S, half, sibling))

    def w_start(out, k, half):
        for way in WAYS:
            out[way, half] = w_send(wrow(0, k), S, half, ydev[way])

    def w_next(copies, out, k, half):
        for way in WAYS:
            got(copies[way, half])
            start, count = CUTS[k][way]
            out[way, half] = w_send(wrow((3, 1)[way], k) + start, count, half, ydev[way])
            to_sibling((3, 1)[way], k, half)

    def w_last(copies, k, half):
        got(copies[0, half], copies[1, half])
        to_sibling(2, k, half)

    def a_next(copies, out, k, d, part, way):
        got(copies[way, part])
        out[way, part] = part_of(a, arow((8 - d, d)[way], k), part, zdev[way])

    def a_start(out, k, part):
        for way in WAYS:
            out[way, part] = part_of(a, arow(0, k), part, zdev[way])

    def a_both(copies, out, k, d, part):
        for way in WAYS:
            a_next(copies, out, k, d, part, way)

    def a_over(dz, part):
        a_l[part].append(part_of(a, arow(dz, 0), part, other_l))

    def a_third(part):
        for way in WAYS:
            if way == part:
                a_next(a2, a3, 0, 3, part, way)
            else:
                got(a2[way, part])
            a_over((5, 3)[way], part)

    def a_fourth(part):
        got(a3[part, part])
        a_over(4, part)

    for n in (0, 1):
        a_x[n] = part_of(a, arow(0, 0), n, other_l)
        a_start(a0, 0, n)
        w_start(w0, 0, n)
        w_x[n] = w_send(wrow(0, 0), S, n, other_h)
    for half in (0, 1):
        to_sibling(0, 0, half)
    a_both(a0, a1, 0, 1, 0)
    w_next(w0, w1, 0, 0)
    a_both(a0, a1, 0, 1, 1)
    a_both(a1, a2, 0, 2, 0)
    got(a_x[0])
    a_start(b0, 1, 0)
    w_next(w0, w1, 0, 1)
    got(w_x[0])
    w_start(v0, 1, 0)
    to_sibling(0, 1, 0)
    a_both(a1, a2, 0, 2, 1)
    got(a_x[1])
    a_start(b0, 1, 1)
    a_third(0)
    got(w_x[1])
    w_start(v0, 1, 1)
    to_sibling(0, 1, 1)
    w_last(w1, 0, 0)
    a_both(b0, b1, 1, 1, 0)
    a_third(1)
    a_fourth(0)
    w_last(w1, 0, 1)
    w_next(v0, v1, 1, 0)
    a_both(b0, b1, 1, 1, 1)
    a_fourth(1)
    w_next(v0, v1, 1, 1)
    w_last(v1, 1, 0)
    got(b1[0, 0], b1[1, 0], *a_l[0], *core_w[0])
    hidden_pass(a, w, g, h, 0, 0)
    w_last(v1, 1, 1)
    got(b1[0, 1], b1[1, 1], *a_l[1])
    hidden_pass(a, w, g, h, 0, 1)

    def sib_row(dy, k):
        return (dp_at(dy, k) // 2) * S

    def yb_row(k, way):
        return (k * 2 + way) * S

    def weight_product(start, half):
        at = rows(start, 2 * S)
        ats = [rows(start + m * D, 2 * S) for m in (0, 1)]
        toks = (slice(0, 256), slice(256, 512))
        first, (gl, gn), (hl, hn) = HALF[half][0], GLANES[half], HLANES[half]
        total = sum(dot(a[r, 0:256], g[t, gl : gl + gn], 1, 0) for r, t in zip(ats, toks))
        p[at, first : first + gn] = total.astype(BF)
        total = sum(dot(a[r, 256:512], h[t, hl : hl + hn], 1, 0) for r, t in zip(ats, toks))
        p[at, first + gn : first + gn + hn] = total.astype(BF)

    def core_copy(dy, k, half, n):
        return pltpu.make_async_remote_copy(
            part(p, wrow(dy, k, 1), S, half), part(sib, sib_row(dy, k), S, half),
            send_sem.at[n], recv_sem.at[n], device_id=sibling, device_id_type=MESH,
        )

    def weight_grads(dys, k, half):
        n0 = len(sent)
        step = (dys[1] - dys[0]) % 4 if len(dys) > 1 else 0
        third = dys[2] - dys[0] - 2 * step if len(dys) > 2 else 0
        for q, dy in enumerate(dys):
            copy = core_copy(dy, k, half, n0 + q)
            sent.append(copy)
            core[dy, k, half] = copy

        @pl.loop(0, len(dys))
        def _(q):
            dy = dys[0] + step * q + third * (q // 2) + 8
            weight_product(sib_row(dy, k) * 2, half)
            core_copy(dy, k, half, n0 + q).start()

    def with_sibling(dy, k, half, *srcs):
        got(core[dy, k, half])
        add_rows(p, wrow(dy, k), S, HALF[half], (sib, sib_row(dy, k)), *srcs)

    def x_far(half):
        with_sibling(2, 1, half)
        far_x[half] = send(part(p, wrow(2, 1), S, half), part(xq, 0, S, half), other_h)

    def y_part(k, way, half, start, count):
        src = part(p, wrow((1, 3)[way], k) + start, count, half)
        return send(src, part(yb, yb_row(k, way) + start, count, half), ydev[way])

    def y_other(half):
        for way in WAYS:
            with_sibling((1, 3)[way], 1, half)
            near1[way, half] = y_part(1, way, half, 0, S)

    def y_near(half):
        for way in WAYS:
            with_sibling((1, 3)[way], 0, half)
            near0[way, half] = y_part(0, way, half, *CUTS[half][1 - way])

    def y_far(half):
        got(far_x[half])
        with_sibling(2, 0, half, (xq, 0))
        for way in WAYS:
            start, count = CUTS[half][way]
            src = part(p, wrow(2, 0) + start, count, half)
            far0[way, half] = send(src, part(ya, way * 80, count, half), ydev[way])

    def y_pass(half):
        for way in WAYS:
            got(far0[way, half])
            start, count = CUTS[half][way]
            to = wrow((1, 3)[way], 0) + start
            add_rows(p, to, count, HALF[half], (ya, way * 80))
            pass0[way, half] = y_part(0, way, half, start, count)

    def x_near(half):
        got(near1[0, half], near1[1, half])
        with_sibling(0, 1, half, (yb, yb_row(1, 0)), (yb, yb_row(1, 1)))
        near_x[half] = send(part(p, wrow(0, 1), S, half), part(xb, 0, S, half), other_h)

    stores = []

    def store(src, dst):
        copy = pltpu.make_async_copy(src, dst, out_sem.at[len(stores)])
        copy.start()
        stores.append(copy)

    def total_of(half):
        got(core[0, 0, half], near_x[half], *(c[way, half] for c in (near0, pass0) for way in WAYS))
        cols = pl.ds(*HALF[half])

        @pl.loop(0, S // 16)
        def _(i):
            total = xb[rows(i * 16, 16), cols].astype(F32)
            for src, start in ((p, wrow(0, 0)), (sib, sib_row(0, 0)), (yb, yb_row(0, 0)),
                               (yb, yb_row(0, 1))):
                total += src[rows(start + i * 16, 16), cols].astype(F32)
            grad_ref[rows(i * 16, 16), cols] = total

        store(grad_ref.at[:, cols], grad_hbm.at[:, cols])

    def input_grad(l_of, pair):
        at = rows((l_of * 4 + pair % 4) * 2 * S, 2 * S)
        total = dot(w[at, 0:512], g[:, 0:512], 1, 1) + dot(w[at, 768:1408], g[:, 512:1152], 1, 1)
        ig[at, :] = total.astype(BF)

    core, far_x, near1, near0, far0, pass0, near_x = {}, {}, {}, {}, {}, {}, {}

    def za_row(k, way, step):
        return ((k * 2 + way) * 3 + step) * S

    def z_far(k):
        out = []
        for way in (0, 1):
            start, count = CUTS[k][way]
            src = ig.at[rows(arow(4, k) + start, count)]
            out.append(send(src, zh.at[rows((k * 2 + way) * 80, count)], zdev[way]))
        return out

    def z_pass(k, copies, d):
        out = []
        for way, dz in enumerate((d, 8 - d)):
            got(copies[way])
            if d == 3:
                start, count = CUTS[k][way]
                add_rows(ig, arow(dz, k) + start, count, (0, T), (zh, (k * 2 + way) * 80))
            else:
                add_rows(ig, arow(dz, k), S, (0, T), (za, za_row(k, way, 2 - d)))
            src = ig.at[rows(arow(dz, k), S)]
            out.append(send(src, za.at[rows(za_row(k, way, 3 - d), S)], zdev[way]))
        return out

    weight_grads((2, 1, 3), 1, 0)
    got(*core_w[1])
    hidden_pass(a, w, g, h, 1, 0)
    x_far(0)
    y_other(0)
    hidden_pass(a, w, g, h, 1, 1)
    far_pair = ((z + 4) % 8) // 2
    zc = {}

    def beside(k):
        @pl.loop(0, 2)
        def _(i):
            input_grad(lk[k], far_pair + 1 + 2 * i)

        zc[k] = z_pass(k, zc[k], 3)

    input_grad(lk[1], far_pair)
    zc[1] = z_far(1)
    weight_grads((2, 1, 3), 1, 1)
    input_grad(lk[0], far_pair)
    zc[0] = z_far(0)
    x_far(1)
    y_other(1)
    beside(1)
    weight_grads((2, 1, 3), 0, 0)
    beside(0)
    y_far(0)
    y_near(0)
    weight_grads((2, 1, 3), 0, 1)
    for half in (0, 1):
        weight_grads((0,), 1, half)
    zc[1] = z_pass(1, zc[1], 2)
    for half in (0, 1):
        weight_grads((0,), 0, half)
    x_near(0)
    y_far(1)
    y_near(1)
    x_near(1)

    @pl.loop(0, 2)
    def _(i):
        input_grad((lo + 1 + i) % 2, far_pair + 2)

    zc[0] = z_pass(0, zc[0], 2)
    y_pass(0)
    zc[1] = z_pass(1, zc[1], 1)
    zc[0] = z_pass(0, zc[0], 1)
    y_pass(1)
    got(*zc[1])
    add_rows(ig, arow(0, 1), S, (0, T), (za, za_row(1, 0, 2)), (za, za_row(1, 1, 2)))
    z_x = send(ig.at[rows(arow(0, 1), S)], xl, other_l)
    total_of(0)

    got(*zc[0], z_x)
    total = ig[rows(arow(0, 0), S), :].astype(F32) + xl[...].astype(F32)
    for way in (0, 1):
        total += za[rows(za_row(0, way, 2), S), :].astype(F32)
    ig_ref[...] = total
    store(ig_ref, ig_hbm)
    total_of(1)
    drain()
    for copy in stores:
        copy.wait()


def moments(m, v, grad):
    m_new = 0.9 * m + 0.1 * grad
    v_new = 0.95 * v + 0.05 * grad * grad
    return m_new, v_new, m_new / (jnp.sqrt(v_new) + 1e-8)


def finish(dp_ref, grad_hbm, ig_hbm, mask_hbm, mgu_hbm, vgu_hbm, md_hbm, vd_hbm,
           out_hbm, mgu_new, vgu_new, sgu_new, md_new, vd_new, sd_new,
           grad_ref, ig_ref, mask, out, old, new, in_sem, out_sem):
    firsts = (mgu_hbm.at[0], mgu_hbm.at[1], md_hbm)
    seconds = (vgu_hbm.at[0], vgu_hbm.at[1], vd_hbm)
    loads = [
        pltpu.make_async_copy(mask_hbm, mask, in_sem.at[6]),
        pltpu.make_async_copy(grad_hbm, grad_ref, in_sem.at[7]),
        pltpu.make_async_copy(ig_hbm, ig_ref, in_sem.at[8]),
    ]
    for k in range(3):
        loads.append(pltpu.make_async_copy(firsts[k], old.at[2 * k], in_sem.at[2 * k]))
        loads.append(pltpu.make_async_copy(seconds[k], old.at[2 * k + 1], in_sem.at[2 * k + 1]))
    for load in loads:
        load.start()
    loads[2].wait()
    out[...] = ig_ref[...].astype(BF)
    stores = [pltpu.make_async_copy(out, out_hbm, out_sem.at[9])]
    stores[0].start()
    loads[0].wait()
    loads[1].wait()
    scale = jnp.float32(8192.0) ** -0.5
    keep = jnp.where(keep_of(mask, dp_ref[0]) != 0, scale, 0.0)
    rest = grad_ref[:, 1280:1408]
    lanes = ((0, 768), (256, 1024), (512, 1408))
    results = ((mgu_new.at[0], vgu_new.at[0], sgu_new.at[0]),
               (mgu_new.at[1], vgu_new.at[1], sgu_new.at[1]),
               (md_new, vd_new, sd_new))
    for k in range(3):
        tail = (rest, pltpu.roll(rest, 64, 1), grad_ref[:, 1664:PK])[k][:, : F - MAIN]
        parts = [grad_ref[:, n : n + 256] for n in lanes[k]]
        grad = jnp.concatenate([*parts, tail], 1)
        loads[3 + 2 * k].wait()
        loads[4 + 2 * k].wait()
        new[3 * k], new[3 * k + 1], new[3 * k + 2] = moments(
            old[2 * k], old[2 * k + 1], grad * keep
        )
        for n in range(3):
            store = pltpu.make_async_copy(new.at[3 * k + n], results[k][n], out_sem.at[3 * k + n])
            store.start()
            stores.append(store)
    for store in stores:
        store.wait()


VMEM = pl.BlockSpec(memory_space=pltpu.VMEM)
HBM = pl.BlockSpec(memory_space=pltpu.HBM)
sds = jax.ShapeDtypeStruct


def ffn(tokens, cotangent, mask, wgu, wd):
    return pl.pallas_call(
        body,
        name="ffn_grads",
        out_shape=(sds((S, PK), F32), sds((S, T), F32)),
        in_specs=[HBM] * 5,
        out_specs=(HBM, HBM),
        scratch_shapes=[
            pltpu.VMEM((S, PK), F32),
            pltpu.VMEM((S, T), F32),
            pltpu.SemaphoreType.DMA((3,)),
            pltpu.VMEM(mask.shape, jnp.int32),
            pltpu.VMEM(wgu.shape, BF),
            pltpu.VMEM(wd.shape, BF),
            pltpu.SemaphoreType.DMA((7,)),
            pltpu.VMEM((2 * D, T), BF),
            pltpu.VMEM((D, PK), BF),
            pltpu.VMEM((D, PK), BF),
            pltpu.VMEM((T, 1152), BF),
            pltpu.VMEM((T, 640), BF),
            pltpu.VMEM((D, T), BF),
            pltpu.VMEM((8 * S, PK), BF),
            pltpu.VMEM((2 * 80, PK), BF),
            pltpu.VMEM((4 * S, PK), BF),
            pltpu.VMEM((S, PK), BF),
            pltpu.VMEM((S, PK), BF),
            pltpu.VMEM((12 * S, T), BF),
            pltpu.VMEM((4 * 80, T), BF),
            pltpu.VMEM((S, T), BF),
            pltpu.SemaphoreType.DMA((COPIES,)),
            pltpu.SemaphoreType.DMA((COPIES,)),
        ],
        compiler_params=pltpu.CompilerParams(
            collective_id=0, has_side_effects=True, vmem_limit_bytes=62 << 20
        ),
    )(tokens, cotangent, mask, wgu, wd)


def on_device(tokens, cotangent, mask, wgu, wd, mgu, vgu, md, vd):
    grad, ig = ffn(tokens.T, cotangent.T, mask, wgu, wd.T)
    dp = lax.axis_index("dp").astype(jnp.int32).reshape(1)
    big, down = sds((2, S, F), F32), sds((S, F), F32)
    out = pl.pallas_call(
        finish,
        name="moments",
        out_shape=(sds((S, T), BF), big, big, big, down, down, down),
        in_specs=[pl.BlockSpec(memory_space=pltpu.SMEM)] + [HBM] * 7,
        out_specs=(HBM,) * 7,
        scratch_shapes=[
            pltpu.VMEM((S, PK), F32),
            pltpu.VMEM((S, T), F32),
            pltpu.VMEM(mask.shape, jnp.int32),
            pltpu.VMEM((S, T), BF),
            pltpu.VMEM((6, S, F), F32),
            pltpu.VMEM((9, S, F), F32),
            pltpu.SemaphoreType.DMA((9,)),
            pltpu.SemaphoreType.DMA((10,)),
        ],
        compiler_params=pltpu.CompilerParams(vmem_limit_bytes=62 << 20),
    )(dp, grad, ig, mask, mgu, vgu, md.T, vd.T)
    return (out[0].T, *out[1:4], *(x.T for x in out[4:]))


def solution(mesh):
    return jax.shard_map(
        on_device,
        mesh=mesh,
        in_specs=(
            P("dp", "tensor"),
            P("dp", "tensor"),
            P(None, "tensor"),
            P(None, "dp", "tensor"),
            P("tensor", "dp"),
            P(None, "dp", "tensor"),
            P(None, "dp", "tensor"),
            P("tensor", "dp"),
            P("tensor", "dp"),
        ),
        out_specs=(
            P("dp", "tensor"),
            P(None, "dp", "tensor"),
            P(None, "dp", "tensor"),
            P(None, "dp", "tensor"),
            P("tensor", "dp"),
            P("tensor", "dp"),
            P("tensor", "dp"),
        ),
        check_vma=False,
    )
```

```python
import functools
import jax
import jax.numpy as jnp
from jax import lax
from jax.experimental import pallas as pl
from jax.experimental.pallas import tpu as pltpu
from jax.sharding import PartitionSpec as P

BF = jnp.bfloat16
F32 = jnp.float32
MESH = pl.DeviceIdType.MESH

D = 2304
S = 144
T = 512
F = 576
MAIN = 512
PK = 1792
HALF = ((0, 768), (768, 1024))
GLANES = ((0, 512), (512, 640))
HLANES = ((0, 256), (256, 384))
CUTS = (((0, 80), (80, 64)), ((80, 64), (0, 80)))
WAYS = (0, 1)
COPIES = 128


def dot(a, b, ca, cb):
    return lax.dot_general(a, b, (((ca,), (cb,)), ((), ())), preferred_element_type=F32)


def rows(start, count, step=16):
    return pl.ds(pl.multiple_of(start, step), count)


def keep_of(mask_ref, dp):
    block = dp + dp // 8
    first = 128 - 16 * (dp % 8)
    row = lax.broadcasted_iota(jnp.int32, (S, F), 0)
    return jnp.where(row < first, mask_ref[pl.ds(block, 1), :], mask_ref[pl.ds(block + 1, 1), :])


def pack(ref, at, keep, gate, up, down):
    gate, up, down = (jnp.where(keep != 0, w.astype(F32), 0.0) for w in (gate, up, down))
    at_lane = 0
    rest = jnp.concatenate([gate[:, MAIN:], up[:, MAIN:]], 1)
    last = jnp.concatenate([down[:, MAIN:], jnp.zeros_like(down[:, MAIN:])], 1)
    for part in (gate[:, :256], up[:, :256], down[:, :256], gate[:, 256:MAIN], up[:, 256:MAIN],
                 rest, down[:, 256:MAIN], last):
        ref[at, at_lane : at_lane + part.shape[1]] = part.astype(BF)
        at_lane += part.shape[1]


def add_rows(dst, to, n, lanes, *srcs):
    cols = pl.ds(*lanes)

    @pl.loop(0, n // 16)
    def _(i):
        at = rows(to + i * 16, 16)
        total = dst[at, cols].astype(F32)
        for src, start in srcs:
            total += src[rows(start + i * 16, 16), cols].astype(F32)
        dst[at, cols] = total.astype(dst.dtype)


def grads_of(gate, up, hidden_grad):
    sig = jax.nn.sigmoid(gate)
    silu = gate * sig
    gate_grad = hidden_grad * up * (sig * (1.0 + gate * (1.0 - sig)))
    return gate_grad, hidden_grad * silu, silu * up


def hidden_pass(a, w, g, h, half, m):
    tok, mine = rows(m * 256, 256, 256), rows(m * D, D, D)
    first, (gl, gn), (hl, hn) = HALF[half][0], GLANES[half], HLANES[half]
    both = dot(a[mine, 0:256], w[:, first : first + gn], 0, 0)
    hg = dot(a[mine, 256:512], w[:, first + gn : first + gn + hn], 0, 0)
    gate_grad, up_grad, hidden = grads_of(both[:, :256], both[:, 256:512], hg[:, :256])
    g[tok, gl : gl + 256] = gate_grad.astype(BF)
    g[tok, gl + 256 : gl + 512] = up_grad.astype(BF)
    h[tok, hl : hl + 256] = hidden.astype(BF)
    if half == 1:
        both, hg = both[:, 512:], hg[:, 256:]
        gate_grad, up_grad, hidden = grads_of(both, pltpu.roll(both, 64, 1), hg)
        low = lax.broadcasted_iota(jnp.int32, (256, 128), 1) < 64
        g[tok, 1024:1152] = jnp.where(low, gate_grad, pltpu.roll(up_grad, 64, 1)).astype(BF)
        h[tok, 512:640] = jnp.where(low, hidden, 0.0).astype(BF)


def body(tok_hbm, cot_hbm, mask_hbm, wgu_hbm, wd_hbm, grad_hbm, ig_hbm,
         grad_ref, ig_ref, out_sem, mask_ref, wgu_ref, wd_ref, in_sem, a, w, p, g, h, ig, sib, ya, yb, xb, xq, za, zh, xl, send_sem, recv_sem):
    dp, tensor = lax.axis_index("dp"), lax.axis_index("tensor")
    y, hi, c = dp // 4, (dp // 2) % 2, dp % 2
    lo, z = tensor // 8, tensor % 8
    hk = (hi, 1 - hi)
    lk = (lo, 1 - lo)

    def dp_at(dy, k, flip=0):
        return (((y + dy) % 4) * 2 + hk[k]) * 2 + (1 - c if flip else c)

    def t_at(dz, k):
        return lk[k] * 8 + (z + dz) % 8

    up_y, down_y = (dp_at(1, 0), tensor), (dp_at(3, 0), tensor)
    up_z, down_z = (dp, t_at(1, 0)), (dp, t_at(7, 0))
    other_h, other_l, sibling = (dp_at(0, 1), tensor), (dp, t_at(0, 1)), (dp_at(0, 0, 1), tensor)
    ydev, zdev = (up_y, down_y), (up_z, down_z)

    moves = [(mask_hbm, mask_ref), (wgu_hbm, wgu_ref), (wd_hbm, wd_ref)]
    for m in (0, 1):
        own = rows((lo * 8 + z) * S + m * D, S)
        for n, src in enumerate((tok_hbm, cot_hbm)):
            moves.append((src.at[:, pl.ds(m * 256, 256)], a.at[own, pl.ds(n * 256, 256)]))
    loads = [pltpu.make_async_copy(*move, in_sem.at[n]) for n, move in enumerate(moves)]
    for load in loads:
        load.start()

    barrier = pltpu.get_barrier_semaphore()
    partners = (up_y, down_y, up_z, down_z, other_h, other_l, sibling)
    for dev in partners:
        pl.semaphore_signal(barrier, inc=1, device_id=dev, device_id_type=MESH)

    sent = []

    def send(src, dst, dev):
        n = len(sent)
        copy = pltpu.make_async_remote_copy(
            src, dst, send_sem.at[n], recv_sem.at[n], device_id=dev, device_id_type=MESH
        )
        copy.start()
        sent.append(copy)
        return copy

    def drain():
        for copy in sent:
            copy.wait_send()

    def got(*copies):
        for copy in copies:
            copy.wait_recv()

    def same(ref, start, count, dev):
        part = ref.at[rows(start, count)]
        return send(part, part, dev)

    def wrow(dy, k, flip=0):
        return dp_at(dy, k, flip) * S

    def arow(dz, k):
        return t_at(dz, k) * S

    def part(ref, start, count, half):
        return ref.at[rows(start, count), pl.ds(*HALF[half])]

    def part_of(ref, start, part, dev):
        return same(ref, start + part * D, S, dev)

    def to_sibling(dy, k):
        w_c.append(same(w, wrow(dy, k), S, sibling))

    for load in loads:
        load.wait()
    pack(w, rows(wrow(0, 0), S), keep_of(mask_ref, dp), wgu_ref[0], wgu_ref[1], wd_ref[...])
    pl.semaphore_wait(barrier, len(partners))
    core_w, a_l = ([], []), ([], [])
    a0, a1, a2, a3, b0, b1, a_x = {}, {}, {}, {}, {}, {}, {}
    w0, w1, v0, v1, w_x = {}, {}, {}, {}, {}

    def w_send(start, count, half, dev):
        src = part(w, start, count, half)
        return send(src, src, dev)

    def to_sibling(dy, k, half):
        core_w[half].append(w_send(wrow(dy, k), S, half, sibling))

    def w_start(out, k, half):
        for way in WAYS:
            out[way, half] = w_send(wrow(0, k), S, half, ydev[way])

    def w_next(copies, out, k, half):
        for way in WAYS:
            got(copies[way, half])
            start, count = CUTS[k][way]
            out[way, half] = w_send(wrow((3, 1)[way], k) + start, count, half, ydev[way])
            to_sibling((3, 1)[way], k, half)

    def w_last(copies, k, half):
        got(copies[0, half], copies[1, half])
        to_sibling(2, k, half)

    def a_next(copies, out, k, d, part, way):
        got(copies[way, part])
        out[way, part] = part_of(a, arow((8 - d, d)[way], k), part, zdev[way])

    def a_start(out, k, part):
        for way in WAYS:
            out[way, part] = part_of(a, arow(0, k), part, zdev[way])

    def a_both(copies, out, k, d, part):
        for way in WAYS:
            a_next(copies, out, k, d, part, way)

    def a_over(dz, part):
        a_l[part].append(part_of(a, arow(dz, 0), part, other_l))

    def a_third(part):
        for way in WAYS:
            if way == part:
                a_next(a2, a3, 0, 3, part, way)
            else:
                got(a2[way, part])
            a_over((5, 3)[way], part)

    def a_fourth(part):
        got(a3[part, part])
        a_over(4, part)

    for n in (0, 1):
        a_x[n] = part_of(a, arow(0, 0), n, other_l)
        a_start(a0, 0, n)
        w_start(w0, 0, n)
        w_x[n] = w_send(wrow(0, 0), S, n, other_h)
    for half in (0, 1):
        to_sibling(0, 0, half)
    a_both(a0, a1, 0, 1, 0)
    w_next(w0, w1, 0, 0)
    a_both(a0, a1, 0, 1, 1)
    a_both(a1, a2, 0, 2, 0)
    got(a_x[0])
    a_start(b0, 1, 0)
    w_next(w0, w1, 0, 1)
    got(w_x[0])
    w_start(v0, 1, 0)
    to_sibling(0, 1, 0)
    a_both(a1, a2, 0, 2, 1)
    got(a_x[1])
    a_start(b0, 1, 1)
    a_third(0)
    got(w_x[1])
    w_start(v0, 1, 1)
    to_sibling(0, 1, 1)
    w_last(w1, 0, 0)
    a_both(b0, b1, 1, 1, 0)
    a_third(1)
    a_fourth(0)
    w_last(w1, 0, 1)
    w_next(v0, v1, 1, 0)
    a_both(b0, b1, 1, 1, 1)
    a_fourth(1)
    w_next(v0, v1, 1, 1)
    w_last(v1, 1, 0)
    got(b1[0, 0], b1[1, 0], *a_l[0], *core_w[0])
    hidden_pass(a, w, g, h, 0, 0)
    w_last(v1, 1, 1)
    got(b1[0, 1], b1[1, 1], *a_l[1])
    hidden_pass(a, w, g, h, 0, 1)

    def sib_row(dy, k):
        return (dp_at(dy, k) // 2) * S

    def yb_row(k, way):
        return (k * 2 + way) * S

    def weight_product(start, half):
        at = rows(start, 2 * S)
        ats = [rows(start + m * D, 2 * S) for m in (0, 1)]
        toks = (slice(0, 256), slice(256, 512))
        first, (gl, gn), (hl, hn) = HALF[half][0], GLANES[half], HLANES[half]
        total = sum(dot(a[r, 0:256], g[t, gl : gl + gn], 1, 0) for r, t in zip(ats, toks))
        p[at, first : first + gn] = total.astype(BF)
        total = sum(dot(a[r, 256:512], h[t, hl : hl + hn], 1, 0) for r, t in zip(ats, toks))
        p[at, first + gn : first + gn + hn] = total.astype(BF)

    def core_copy(dy, k, half, n):
        return pltpu.make_async_remote_copy(
            part(p, wrow(dy, k, 1), S, half), part(sib, sib_row(dy, k), S, half),
            send_sem.at[n], recv_sem.at[n], device_id=sibling, device_id_type=MESH,
        )

    def weight_grads(dys, k, half):
        n0 = len(sent)
        step = (dys[1] - dys[0]) % 4 if len(dys) > 1 else 0
        third = dys[2] - dys[0] - 2 * step if len(dys) > 2 else 0
        for q, dy in enumerate(dys):
            copy = core_copy(dy, k, half, n0 + q)
            sent.append(copy)
            core[dy, k, half] = copy

        @pl.loop(0, len(dys))
        def _(q):
            dy = dys[0] + step * q + third * (q // 2) + 8
            weight_product(sib_row(dy, k) * 2, half)
            core_copy(dy, k, half, n0 + q).start()

    def with_sibling(dy, k, half, *srcs):
        got(core[dy, k, half])
        add_rows(p, wrow(dy, k), S, HALF[half], (sib, sib_row(dy, k)), *srcs)

    def x_far(half):
        with_sibling(2, 1, half)
        far_x[half] = send(part(p, wrow(2, 1), S, half), part(xq, 0, S, half), other_h)

    def y_part(k, way, half, start, count):
        src = part(p, wrow((1, 3)[way], k) + start, count, half)
        return send(src, part(yb, yb_row(k, way) + start, count, half), ydev[way])

    def y_other(half):
        for way in WAYS:
            with_sibling((1, 3)[way], 1, half)
            near1[way, half] = y_part(1, way, half, 0, S)

    def y_near(half):
        for way in WAYS:
            with_sibling((1, 3)[way], 0, half)
            near0[way, half] = y_part(0, way, half, *CUTS[half][1 - way])

    def y_far(half):
        got(far_x[half])
        with_sibling(2, 0, half, (xq, 0))
        for way in WAYS:
            start, count = CUTS[half][way]
            src = part(p, wrow(2, 0) + start, count, half)
            far0[way, half] = send(src, part(ya, way * 80, count, half), ydev[way])

    def y_pass(half):
        for way in WAYS:
            got(far0[way, half])
            start, count = CUTS[half][way]
            to = wrow((1, 3)[way], 0) + start
            add_rows(p, to, count, HALF[half], (ya, way * 80))
            pass0[way, half] = y_part(0, way, half, start, count)

    def x_near(half):
        got(near1[0, half], near1[1, half])
        with_sibling(0, 1, half, (yb, yb_row(1, 0)), (yb, yb_row(1, 1)))
        near_x[half] = send(part(p, wrow(0, 1), S, half), part(xb, 0, S, half), other_h)

    stores = []

    def store(src, dst):
        copy = pltpu.make_async_copy(src, dst, out_sem.at[len(stores)])
        copy.start()
        stores.append(copy)

    def total_of(half):
        got(core[0, 0, half], near_x[half], *(c[way, half] for c in (near0, pass0) for way in WAYS))
        cols = pl.ds(*HALF[half])

        @pl.loop(0, S // 16)
        def _(i):
            total = xb[rows(i * 16, 16), cols].astype(F32)
            for src, start in ((p, wrow(0, 0)), (sib, sib_row(0, 0)), (yb, yb_row(0, 0)),
                               (yb, yb_row(0, 1))):
                total += src[rows(start + i * 16, 16), cols].astype(F32)
            grad_ref[rows(i * 16, 16), cols] = total

        store(grad_ref.at[:, cols], grad_hbm.at[:, cols])

    def input_grad(l_of, pair):
        at = rows((l_of * 4 + pair % 4) * 2 * S, 2 * S)
        total = dot(w[at, 0:512], g[:, 0:512], 1, 1) + dot(w[at, 768:1408], g[:, 512:1152], 1, 1)
        ig[at, :] = total.astype(BF)

    core, far_x, near1, near0, far0, pass0, near_x = {}, {}, {}, {}, {}, {}, {}

    def za_row(k, way, step):
        return ((k * 2 + way) * 3 + step) * S

    def z_far(k):
        out = []
        for way in (0, 1):
            start, count = CUTS[k][way]
            src = ig.at[rows(arow(4, k) + start, count)]
            out.append(send(src, zh.at[rows((k * 2 + way) * 80, count)], zdev[way]))
        return out

    def z_pass(k, copies, d):
        out = []
        for way, dz in enumerate((d, 8 - d)):
            got(copies[way])
            if d == 3:
                start, count = CUTS[k][way]
                add_rows(ig, arow(dz, k) + start, count, (0, T), (zh, (k * 2 + way) * 80))
            else:
                add_rows(ig, arow(dz, k), S, (0, T), (za, za_row(k, way, 2 - d)))
            src = ig.at[rows(arow(dz, k), S)]
            out.append(send(src, za.at[rows(za_row(k, way, 3 - d), S)], zdev[way]))
        return out

    weight_grads((2, 1, 3), 1, 0)
    got(*core_w[1])
    hidden_pass(a, w, g, h, 1, 0)
    x_far(0)
    y_other(0)
    hidden_pass(a, w, g, h, 1, 1)
    far_pair = ((z + 4) % 8) // 2
    zc = {}

    def beside(k):
        @pl.loop(0, 2)
        def _(i):
            input_grad(lk[k], far_pair + 1 + 2 * i)

        zc[k] = z_pass(k, zc[k], 3)

    input_grad(lk[1], far_pair)
    zc[1] = z_far(1)
    weight_grads((2, 1, 3), 1, 1)
    input_grad(lk[0], far_pair)
    zc[0] = z_far(0)
    x_far(1)
    y_other(1)
    beside(1)
    weight_grads((2, 1, 3), 0, 0)
    beside(0)
    y_far(0)
    y_near(0)
    weight_grads((2, 1, 3), 0, 1)
    for half in (0, 1):
        weight_grads((0,), 1, half)
    zc[1] = z_pass(1, zc[1], 2)
    for half in (0, 1):
        weight_grads((0,), 0, half)
    x_near(0)
    y_far(1)
    y_near(1)
    x_near(1)

    @pl.loop(0, 2)
    def _(i):
        input_grad((lo + 1 + i) % 2, far_pair + 2)

    zc[0] = z_pass(0, zc[0], 2)
    y_pass(0)
    zc[1] = z_pass(1, zc[1], 1)
    zc[0] = z_pass(0, zc[0], 1)
    y_pass(1)
    got(*zc[1])
    add_rows(ig, arow(0, 1), S, (0, T), (za, za_row(1, 0, 2)), (za, za_row(1, 1, 2)))
    z_x = send(ig.at[rows(arow(0, 1), S)], xl, other_l)
    total_of(0)

    got(*zc[0], z_x)
    total = ig[rows(arow(0, 0), S), :].astype(F32) + xl[...].astype(F32)
    for way in (0, 1):
        total += za[rows(za_row(0, way, 2), S), :].astype(F32)
    ig_ref[...] = total.astype(BF)
    store(ig_ref, ig_hbm)
    total_of(1)
    drain()
    for copy in stores:
        copy.wait()


def moments(m, v, grad):
    m_new = 0.9 * m + 0.1 * grad
    v_new = 0.95 * v + 0.05 * grad * grad
    return m_new, v_new, m_new / (jnp.sqrt(v_new) + 1e-8)


def finish(dp_ref, grad_hbm, ig_hbm, mask_hbm, mgu_hbm, vgu_hbm, md_hbm, vd_hbm,
           out_hbm, mgu_new, vgu_new, sgu_new, md_new, vd_new, sd_new,
           grad_ref, mask, old, new, in_sem, out_sem):
    firsts = (mgu_hbm.at[0], mgu_hbm.at[1], md_hbm)
    seconds = (vgu_hbm.at[0], vgu_hbm.at[1], vd_hbm)
    loads = [
        pltpu.make_async_copy(mask_hbm, mask, in_sem.at[6]),
        pltpu.make_async_copy(grad_hbm, grad_ref, in_sem.at[7]),
    ]
    for k in range(3):
        loads.append(pltpu.make_async_copy(firsts[k], old.at[2 * k], in_sem.at[2 * k]))
        loads.append(pltpu.make_async_copy(seconds[k], old.at[2 * k + 1], in_sem.at[2 * k + 1]))
    for load in loads:
        load.start()
    stores = [pltpu.make_async_copy(ig_hbm, out_hbm, out_sem.at[9])]
    stores[0].start()
    loads[0].wait()
    loads[1].wait()
    scale = jnp.float32(8192.0) ** -0.5
    keep = jnp.where(keep_of(mask, dp_ref[0]) != 0, scale, 0.0)
    rest = grad_ref[:, 1280:1408]
    lanes = ((0, 768), (256, 1024), (512, 1408))
    results = ((mgu_new.at[0], vgu_new.at[0], sgu_new.at[0]),
               (mgu_new.at[1], vgu_new.at[1], sgu_new.at[1]),
               (md_new, vd_new, sd_new))
    for k in range(3):
        tail = (rest, pltpu.roll(rest, 64, 1), grad_ref[:, 1664:PK])[k][:, : F - MAIN]
        parts = [grad_ref[:, n : n + 256] for n in lanes[k]]
        grad = jnp.concatenate([*parts, tail], 1)
        loads[2 + 2 * k].wait()
        loads[3 + 2 * k].wait()
        new[3 * k], new[3 * k + 1], new[3 * k + 2] = moments(
            old[2 * k], old[2 * k + 1], grad * keep
        )
        for n in range(3):
            store = pltpu.make_async_copy(new.at[3 * k + n], results[k][n], out_sem.at[3 * k + n])
            store.start()
            stores.append(store)
    for store in stores:
        store.wait()


VMEM = pl.BlockSpec(memory_space=pltpu.VMEM)
HBM = pl.BlockSpec(memory_space=pltpu.HBM)
sds = jax.ShapeDtypeStruct


def ffn(tokens, cotangent, mask, wgu, wd):
    return pl.pallas_call(
        body,
        name="ffn_grads",
        out_shape=(sds((S, PK), F32), sds((S, T), BF)),
        in_specs=[HBM] * 5,
        out_specs=(HBM, HBM),
        scratch_shapes=[
            pltpu.VMEM((S, PK), F32),
            pltpu.VMEM((S, T), BF),
            pltpu.SemaphoreType.DMA((3,)),
            pltpu.VMEM(mask.shape, jnp.int32),
            pltpu.VMEM(wgu.shape, BF),
            pltpu.VMEM(wd.shape, BF),
            pltpu.SemaphoreType.DMA((7,)),
            pltpu.VMEM((2 * D, T), BF),
            pltpu.VMEM((D, PK), BF),
            pltpu.VMEM((D, PK), BF),
            pltpu.VMEM((T, 1152), BF),
            pltpu.VMEM((T, 640), BF),
            pltpu.VMEM((D, T), BF),
            pltpu.VMEM((8 * S, PK), BF),
            pltpu.VMEM((2 * 80, PK), BF),
            pltpu.VMEM((4 * S, PK), BF),
            pltpu.VMEM((S, PK), BF),
            pltpu.VMEM((S, PK), BF),
            pltpu.VMEM((12 * S, T), BF),
            pltpu.VMEM((4 * 80, T), BF),
            pltpu.VMEM((S, T), BF),
            pltpu.SemaphoreType.DMA((COPIES,)),
            pltpu.SemaphoreType.DMA((COPIES,)),
        ],
        compiler_params=pltpu.CompilerParams(
            collective_id=0, has_side_effects=True, vmem_limit_bytes=62 << 20
        ),
    )(tokens, cotangent, mask, wgu, wd)


def on_device(tokens, cotangent, mask, wgu, wd, mgu, vgu, md, vd):
    grad, ig = ffn(tokens.T, cotangent.T, mask, wgu, wd.T)
    dp = lax.axis_index("dp").astype(jnp.int32).reshape(1)
    big, down = sds((2, S, F), F32), sds((S, F), F32)
    out = pl.pallas_call(
        finish,
        name="moments",
        out_shape=(sds((S, T), BF), big, big, big, down, down, down),
        in_specs=[pl.BlockSpec(memory_space=pltpu.SMEM)] + [HBM] * 7,
        out_specs=(HBM,) * 7,
        scratch_shapes=[
            pltpu.VMEM((S, PK), F32),
            pltpu.VMEM(mask.shape, jnp.int32),
            pltpu.VMEM((6, S, F), F32),
            pltpu.VMEM((9, S, F), F32),
            pltpu.SemaphoreType.DMA((8,)),
            pltpu.SemaphoreType.DMA((10,)),
        ],
        compiler_params=pltpu.CompilerParams(vmem_limit_bytes=62 << 20),
    )(dp, grad, ig, mask, mgu, vgu, md.T, vd.T)
    return (out[0].T, *out[1:4], *(x.T for x in out[4:]))


def solution(mesh):
    return jax.shard_map(
        on_device,
        mesh=mesh,
        in_specs=(
            P("dp", "tensor"),
            P("dp", "tensor"),
            P(None, "tensor"),
            P(None, "dp", "tensor"),
            P("tensor", "dp"),
            P(None, "dp", "tensor"),
            P(None, "dp", "tensor"),
            P("tensor", "dp"),
            P("tensor", "dp"),
        ),
        out_specs=(
            P("dp", "tensor"),
            P(None, "dp", "tensor"),
            P(None, "dp", "tensor"),
            P(None, "dp", "tensor"),
            P("tensor", "dp"),
            P("tensor", "dp"),
            P("tensor", "dp"),
        ),
        check_vma=False,
    )
```
